32 devices in a mesh: seq: 8 (over z, x), fsdp: 4 (over y, core).
Axes of the slice: x: 2, y: 2, z: 4, core: 2. Of those that a mesh axis runs over, the one named last changes fastest.
Arguments:
- tokens: bfloat16 [4, 1024, 2048], P('fsdp', 'seq'), may hold values from -6 to 6
- block_pos: int32 [4, 8], P('fsdp'), may hold values from 0 to 7, each once within a row
- w_query: bfloat16 [2048, 2048], P(('seq', 'fsdp')), may hold values from -0.125 to 0.125
- key_weight: bfloat16 [2048, 1024], P(('seq', 'fsdp')), may hold values from -0.125 to 0.125
- value_weight: bfloat16 [2048, 1024], P(('seq', 'fsdp')), may hold values from -0.125 to 0.125
- w_out: bfloat16 [2048, 2048], P(('seq', 'fsdp')), may hold values from -0.375 to 0.375
- w_gate: bfloat16 [2048, 6144], P(('seq', 'fsdp')), may hold values from -0.125 to 0.125
- w_up: bfloat16 [2048, 6144], P(('seq', 'fsdp')), may hold values from -0.125 to 0.125
- w_down: bfloat16 [2048, 6144], P(('seq', 'fsdp')), may hold values from -0.15625 to 0.15625
- attn_gain: bfloat16 [2048], P(('seq', 'fsdp')), may hold values from 0.099609375 to 1.8984375
- mlp_gain: bfloat16 [2048], P(('seq', 'fsdp')), may hold values from 0.099609375 to 1.8984375
- qk_gain: bfloat16 [2, 128], P(None, ('seq', 'fsdp')), may hold values from 0.099609375 to 1.8984375
- grad_out: bfloat16 [4, 1024, 2048], P('fsdp', 'seq'), may hold values from -6 to 6
Outputs:
- output: bfloat16 [4, 1024, 2048], P('fsdp', 'seq')
- grad_tokens: float32 [4, 1024, 2048], P('fsdp', 'seq')
- grad_query: float32 [2048, 2048], P(('seq', 'fsdp'))
- grad_key: float32 [2048, 1024], P(('seq', 'fsdp'))
- grad_value: float32 [2048, 1024], P(('seq', 'fsdp'))
- grad_outproj: float32 [2048, 2048], P(('seq', 'fsdp'))
- grad_gate: float32 [2048, 6144], P(('seq', 'fsdp'))
- grad_up: float32 [2048, 6144], P(('seq', 'fsdp'))
- grad_down: float32 [2048, 6144], P(('seq', 'fsdp'))
- grad_attn_gain: float32 [2048], P(('seq', 'fsdp'))
- grad_mlp_gain: float32 [2048], P(('seq', 'fsdp'))
- grad_qk_gain: float32 [2, 128], P(None, ('seq', 'fsdp'))
The draws below stay inside these ranges and needn't reach their ends.
Inputs may be any that keep to these rules, and one draw needn't show every extreme that they name: Each row of block_pos is a permutation: index s of seq holds positions block_pos[f, s] * 128 to block_pos[f, s] * 128 + 127 of sequence f.
All inputs are finite; a program needn't handle non-finite values.
Results may differ from the reference program's by a relative error of at most 0.02.
Values may be sent and summed in bfloat16 or wider, within the bound.
No kernel may reach another device: no remote copies, remote signals or barrier semaphores. Data moves between devices by JAX's collectives and lax.ppermute only.
A program may use at most 640 MiB of HBM per device.

```python
import jax
import jax.numpy as jnp
from jax import lax

MODEL_WIDTH = 2048
QUERY_HEADS = 16
KEY_VALUE_HEADS = 8
HEAD_SIZE = 128
FF = 6144
TOK_DEV = 128
SEQS = 4
SEQUENCE_LENGTH = 1024
N_SEQ = 8


def spiked(entries, own_key, source, target, shards_of, factor):
    owner, partner = [(jnp.arange(entries.shape[axis_at]) // (entries.shape[axis_at] // shards_of)).reshape([-1 if axis == axis_at else 1 for axis in range(entries.ndim)]) for axis_at in (source, target)]
    chosen = jax.random.permutation(own_key, shards_of)[partner]
    strong = (owner == chosen) | (owner == (partner + shards_of // 2) % shards_of)
    return jnp.where(strong, factor * entries, entries)


def block_scale(stream_key, shape, shards, low, largest):
    def one(axis_at, parts):
        draws = jax.random.uniform(jax.random.fold_in(jax.random.fold_in(stream_key, 6), axis_at), (parts,), jnp.float32, low / len(shards), largest / len(shards))
        return jnp.repeat(jnp.exp(draws), shape[axis_at] // parts).reshape((-1,) + (1,) * (len(shape) - axis_at - 1))

    level = one(*shards[0])
    for cut in shards[1:]:
        level = level * one(*cut)
    return level


def bell_draw(key, extent, scale, most, cuts=(), kind=jnp.bfloat16):
    loudness = block_scale(key, extent, cuts, -0.22, 0.18) if cuts else 1.0
    array = jax.random.normal(key, extent, jnp.float32) * scale * loudness
    return jnp.minimum(jnp.maximum(array, -most), most).astype(kind)


def noise_with(rng, extent, scale, reach, cuts, heavy, kind=jnp.bfloat16):
    drawn = scale * jax.random.normal(rng, extent, jnp.float32)
    if cuts:
        drawn = drawn * block_scale(rng, extent, cuts, -0.22, 0.18)
    return jnp.clip(spiked(drawn, jax.random.fold_in(rng, 3), *heavy), -reach, reach).astype(kind)


def setup_inputs(seed: int = 0) -> dict:
    splits = jax.random.split(jax.random.key(seed), 14)
    tokens = noise_with(splits[0], (SEQS, SEQUENCE_LENGTH, MODEL_WIDTH), 1.0, 6.0, ((0, 4), (1, 8)), (1, 2, 8, 2.0))
    block_pos = jax.vmap(lambda own: jax.random.permutation(own, N_SEQ))(jax.random.split(splits[1], SEQS)).reshape((SEQS, N_SEQ)).astype(jnp.int32)
    w_query = bell_draw(splits[2], (MODEL_WIDTH, QUERY_HEADS * HEAD_SIZE), MODEL_WIDTH ** -0.5, 0.125, ((0, 32),))
    key_weight = bell_draw(splits[3], (MODEL_WIDTH, KEY_VALUE_HEADS * HEAD_SIZE), MODEL_WIDTH ** -0.5, 0.125, ((0, 32),))
    value_weight = bell_draw(splits[4], (MODEL_WIDTH, KEY_VALUE_HEADS * HEAD_SIZE), MODEL_WIDTH ** -0.5, 0.125, ((0, 32),))
    w_out = bell_draw(splits[5], (MODEL_WIDTH, QUERY_HEADS * HEAD_SIZE), (QUERY_HEADS * HEAD_SIZE // 8) ** -0.5, 0.375, ((0, 32),))
    w_gate = bell_draw(splits[6], (MODEL_WIDTH, FF), MODEL_WIDTH ** -0.5, 0.125, ((0, 32),))
    w_up = bell_draw(splits[7], (MODEL_WIDTH, FF), MODEL_WIDTH ** -0.5, 0.125, ((0, 32),))
    w_down = bell_draw(splits[8], (MODEL_WIDTH, FF), (FF // 4) ** -0.5, 0.15625, ((0, 32),))
    attn_gain = jnp.clip(1.0 + 0.18 * jax.random.normal(splits[9], (MODEL_WIDTH,), jnp.float32), 0.099609375, 1.8984375).astype(jnp.bfloat16)
    mlp_gain = jnp.clip(1.0 + 0.18 * jax.random.normal(splits[10], (MODEL_WIDTH,), jnp.float32), 0.099609375, 1.8984375).astype(jnp.bfloat16)
    qk_gain = jnp.clip(1.0 + 0.18 * jax.random.normal(splits[11], (2, HEAD_SIZE), jnp.float32), 0.099609375, 1.8984375).astype(jnp.bfloat16)
    grad_out = noise_with(splits[12], (SEQS, SEQUENCE_LENGTH, MODEL_WIDTH), 1.0, 6.0, ((0, 4), (1, 8)), (1, 2, 8, 2.0))
    return {"tokens": tokens, "block_pos": block_pos, "w_query": w_query, "key_weight": key_weight, "value_weight": value_weight, "w_out": w_out, "w_gate": w_gate, "w_up": w_up, "w_down": w_down, "attn_gain": attn_gain, "mlp_gain": mlp_gain, "qk_gain": qk_gain, "grad_out": grad_out}


rope_base = 1000000.0
norm_eps = 1e-06
highest = lax.Precision.HIGHEST

@jax.custom_vjp
def low(v):
    return lax.optimization_barrier(v.astype(jnp.bfloat16)).astype(jnp.float32)

@jax.custom_vjp
def lower_backward(v):
    return v

def low_keep(v):
    return (low(v), None)

def low_pass(kept, grad):
    return (grad,)

def back_keep(v):
    return (v, None)

def back_low(kept, grad):
    return (low(grad),)
low.defvjp(low_keep, low_pass)
lower_backward.defvjp(back_keep, back_low)

def forward_and_backward(tensor):
    return lower_backward(low(tensor))

def matrix_product(left, right):
    return jnp.dot(left, right, precision=highest, preferred_element_type=jnp.float32)

def matmul_t(left, right):
    return lax.dot_general(left, right, (((1,), (1,)), ((), ())), precision=highest, preferred_element_type=jnp.float32)

def rms_norm(tensor, gain):
    return tensor * lax.rsqrt(lax.optimization_barrier(jnp.mean(tensor * tensor, axis=-1, keepdims=True)) + norm_eps) * gain

def rope_angles(positions):
    exponent = jnp.arange(HEAD_SIZE // 2, dtype=jnp.float32) * (-2.0 / HEAD_SIZE)
    frequency = rope_base ** exponent
    return positions.astype(jnp.float32)[:, None] * frequency[None, :]

def rotate(tensor, angles):
    half_width = tensor.shape[-1] // 2
    cosine = jnp.cos(angles)[:, None, :]
    sine_part = jnp.sin(angles)[:, None, :]
    front_half = tensor[..., :half_width]
    back_half = tensor[..., half_width:]
    return jnp.concatenate([front_half * cosine - back_half * sine_part, back_half * cosine + front_half * sine_part], axis=-1)

def attention(query_rows, rotated_keys, values, positions):
    queries_per_group = QUERY_HEADS // KEY_VALUE_HEADS
    rows_per_block = min(512, SEQUENCE_LENGTH)
    position_block_count = SEQUENCE_LENGTH // rows_per_block
    score_scale = HEAD_SIZE ** (-0.5)
    query_position_blocks = query_rows.reshape(position_block_count, rows_per_block, KEY_VALUE_HEADS, queries_per_group, HEAD_SIZE)
    position_blocks = positions.reshape(position_block_count, rows_per_block)

    def one_block(pieces):
        query_block, query_pos = pieces
        scores = jnp.einsum('qkgd,tkd->kgqt', query_block, rotated_keys, precision=highest) * score_scale
        scores = lower_backward(scores)
        visible = query_pos[:, None] >= positions[None, :]
        scores = jnp.where(visible, scores, -1e+30)
        row_top = lax.optimization_barrier(jnp.max(scores, axis=-1, keepdims=True))
        weights = jnp.exp(scores - row_top)
        weights = weights / lax.optimization_barrier(jnp.sum(weights, axis=-1, keepdims=True))
        mixed = jnp.einsum('kgqt,tkd->qkgd', low(weights), values, precision=highest)
        return mixed.reshape(rows_per_block, QUERY_HEADS * HEAD_SIZE)
    results = lax.map(jax.checkpoint(one_block), (query_position_blocks, position_blocks))
    return results.reshape(SEQUENCE_LENGTH, QUERY_HEADS * HEAD_SIZE)

def layer(hidden_in, positions, w_query, key_weight, value_weight, w_out, w_gate, w_up, w_down, attn_gain, mlp_gain, qk_gain):
    angles = rope_angles(positions)
    normalized_input = low(rms_norm(hidden_in, attn_gain))
    q_pre = lower_backward(matrix_product(normalized_input, w_query)).reshape(SEQUENCE_LENGTH, QUERY_HEADS, HEAD_SIZE)
    key_before_rotation = lower_backward(matrix_product(normalized_input, key_weight)).reshape(SEQUENCE_LENGTH, KEY_VALUE_HEADS, HEAD_SIZE)
    value_matrix_rows = forward_and_backward(matrix_product(normalized_input, value_weight)).reshape(SEQUENCE_LENGTH, KEY_VALUE_HEADS, HEAD_SIZE)
    query_rows = low(rotate(rms_norm(q_pre, qk_gain[0]), angles))
    rotated_keys = low(rotate(rms_norm(key_before_rotation, qk_gain[1]), angles))
    attended = forward_and_backward(attention(query_rows, rotated_keys, value_matrix_rows, positions))
    branch = lower_backward(matmul_t(attended, w_out))
    middle = hidden_in + branch
    normed2 = low(rms_norm(middle, mlp_gain))
    gate_act = lower_backward(matrix_product(normed2, w_gate))
    up_act = lower_backward(matrix_product(normed2, w_up))
    inner = low(jax.nn.silu(gate_act) * up_act)
    return middle + matmul_t(inner, w_down)

def reference(tokens, block_pos, w_query, key_weight, value_weight, w_out, w_gate, w_up, w_down, attn_gain, mlp_gain, qk_gain, grad_out):
    offsets = jnp.arange(TOK_DEV, dtype=jnp.int32)
    positions = (block_pos[:, :, None] * TOK_DEV + offsets[None, None, :]).reshape(SEQS, SEQUENCE_LENGTH).astype(jnp.int32)
    floats = [tensor.astype(jnp.float32) for tensor in (tokens, w_query, key_weight, value_weight, w_out, w_gate, w_up, w_down, attn_gain, mlp_gain, qk_gain)]

    def forward(tokens_f, *weights):

        def per_sequence(pieces):
            return layer(pieces[0], pieces[1], *weights)
        return lax.map(per_sequence, (tokens_f, positions))
    result, pullback = jax.vjp(forward, *floats)
    grads = pullback(grad_out.astype(jnp.float32))
    return (result.astype(jnp.bfloat16), grads[0], grads[1], grads[2], grads[3], grads[4], grads[5], grads[6], grads[7], grads[8], grads[9], grads[10])
```

```python
import jax
import jax.numpy as jnp
from jax import lax
from jax.sharding import PartitionSpec as P

QUERY_HEADS = 16
KEY_VALUE_HEADS = 8
HEAD_SIZE = 128
FF = 6144

rope_base = 1000000.0
norm_eps = 1e-06
BOTH = ("seq", "fsdp")
bf16 = jnp.bfloat16
f32 = jnp.float32

PARTS = KEY_VALUE_HEADS // 2
GROUP = QUERY_HEADS // KEY_VALUE_HEADS


def dot(left, right):
    return jnp.dot(left, right, preferred_element_type=f32)


def dot_t(left, right):
    return lax.dot_general(left, right, (((1,), (1,)), ((), ())), preferred_element_type=f32)


def dot_tn(left, right):
    return lax.dot_general(left, right, (((0,), (0,)), ((), ())), preferred_element_type=f32)


def inv_rms(tensor):
    return lax.rsqrt(jnp.mean(tensor * tensor, axis=-1, keepdims=True) + norm_eps)


def norm_back(tensor, root, gain, incoming):
    scaled = gain * incoming
    return root * scaled - tensor * (root * root * root) * jnp.mean(
        scaled * tensor, axis=-1, keepdims=True
    )


def halves(tensor):
    half_width = tensor.shape[-1] // 2
    return tensor[..., :half_width], tensor[..., half_width:]


def rotate(tensor, cosine, sine):
    front, back = halves(tensor)
    return jnp.concatenate([front * cosine - back * sine, back * cosine + front * sine], axis=-1)


def unrotate(tensor, cosine, sine):
    front, back = halves(tensor)
    return jnp.concatenate([front * cosine + back * sine, back * cosine - front * sine], axis=-1)


class Grid:
    def __init__(self):
        self.seq = lax.axis_size("seq")
        self.fsdp = lax.axis_size("fsdp")
        self.A = PARTS
        self.R = self.seq // self.A
        self.Y = self.fsdp // 2
        s, f = lax.axis_index("seq"), lax.axis_index("fsdp")
        self.a, self.b = s // self.R, s % self.R
        self.y, self.c = f // 2, f % 2
        self.places = [
            (a, b, y, c)
            for a in range(self.A)
            for b in range(self.R)
            for y in range(self.Y)
            for c in range(2)
        ]

    def at(self, a, b, y, c):
        return ((a % self.A) * self.R + b % self.R) * self.fsdp + (y % self.Y) * 2 + c % 2

    def move(self, array, a=0, b=0, y=0, c=0):
        route = [
            (self.at(*p), self.at(p[0] + a, p[1] + b, p[2] + y, p[3] + c)) for p in self.places
        ]
        return lax.ppermute(array, BOTH, route)

    def swap(self, array):
        return self.move(array, c=1)

    def exchange_a(self, array):
        groups = [
            [self.at(a, b, y, c) for a in range(self.A)]
            for b in range(self.R)
            for y in range(self.Y)
            for c in range(2)
        ]
        return lax.all_to_all(array, BOTH, 0, 0, axis_index_groups=groups, tiled=True)

    def ring_a(self, array):
        held = [array]
        for _ in range(self.A - 1):
            held.append(self.move(held[-1], a=1))
        return held

    def by_core(self, first, second):
        return (
            jnp.where(self.c == 0, first, second),
            jnp.where(self.c == 0, second, first),
        )

    def spread(self, piece, b_first):
        got = {(0, 0): piece}
        if b_first:
            for i in range(1, self.R):
                got[i, 0] = self.move(piece, b=i)
            for i in range(self.R):
                for j in range(1, self.Y):
                    got[i, j] = self.move(got[i, 0], y=j)
        else:
            for j in range(1, self.Y):
                got[0, j] = self.move(piece, y=j)
            for j in range(self.Y):
                for i in range(1, self.R):
                    got[i, j] = self.move(got[0, j], b=i)
        return [got[i, j] for i in range(self.R) for j in range(self.Y)]

    def collect(self, pieces, b_first, wide=False):
        held = {
            (i, j): pieces[i * self.Y + j] for i in range(self.R) for j in range(self.Y)
        }
        sent = (lambda v: v) if wide else (lambda v: v.astype(bf16))
        if b_first:
            rows = {}
            for j in reversed(range(self.Y)):
                total = held[0, j].astype(f32)
                for i in range(1, self.R):
                    total = total + self.move(sent(held[i, j]), b=-i).astype(f32)
                rows[j] = total
            total = rows[0]
            for j in range(1, self.Y):
                total = total + self.move(sent(rows[j]), y=-j).astype(f32)
            return total
        columns = {}
        for i in reversed(range(self.R)):
            total = held[i, 0].astype(f32)
            for j in range(1, self.Y):
                total = total + self.move(sent(held[i, j]), y=-j).astype(f32)
            columns[i] = total
        total = columns[0]
        for i in range(1, self.R):
            total = total + self.move(sent(columns[i]), b=-i).astype(f32)
        return total

    def sum_over_a(self, partial, rows):
        total = partial[:rows].astype(f32)
        for d in range(1, self.A):
            block = partial[d * rows : (d + 1) * rows].astype(bf16)
            total = total + self.move(block, a=-d).astype(f32)
        return total


def on_device(
    tokens,
    block_pos,
    w_query,
    key_weight,
    value_weight,
    w_out,
    w_gate,
    w_up,
    w_down,
    attn_gain,
    mlp_gain,
    qk_gain,
    grad_out,
):
    g = Grid()
    A, R, Y = g.A, g.R, g.Y
    a, b, y, c = g.a, g.b, g.y, g.c
    pieces = R * Y
    rows_own = w_query.shape[0]
    width = tokens.shape[2]
    piece_width = width // pieces
    token_rows = tokens.shape[1]
    group_rows = A * token_rows
    score_scale = HEAD_SIZE ** (-0.5)
    q_cols = GROUP * HEAD_SIZE
    ff_cols = FF // (2 * A)

    def permuted(rows):
        split = rows.reshape(rows.shape[0], A, R, Y, 2 * rows_own)
        split = jnp.transpose(split, (2, 3, 0, 1, 4)).reshape(R, Y, rows.shape[0], piece_width)
        split = jnp.stack([split[(b - i) % R] for i in range(R)])
        split = jnp.stack([split[:, (y - j) % Y] for j in range(Y)], axis=1)
        return jnp.concatenate([split[i, j] for i in range(R) for j in range(Y)], axis=1)

    def restored(rows):
        split = rows.reshape(rows.shape[0], R, Y, piece_width)
        split = jnp.transpose(split, (1, 2, 0, 3))
        split = jnp.stack([split[(b - i) % R] for i in range(R)])
        split = jnp.stack([split[:, (y - j) % Y] for j in range(Y)], axis=1)
        split = split.reshape(R, Y, rows.shape[0], A, 2 * rows_own)
        return jnp.transpose(split, (2, 3, 0, 1, 4)).reshape(rows.shape[0], width)

    def cut(array, i):
        return array[:, i * piece_width : (i + 1) * piece_width]

    def own_and_other(local):
        turned = jnp.transpose(local, (2, 1, 0, 3))
        keep = lax.dynamic_index_in_dim(turned, c, 0, keepdims=False)
        send = lax.dynamic_index_in_dim(turned, 1 - c, 0, keepdims=False)
        low, high = g.by_core(keep, g.swap(send))
        return jnp.concatenate([low, high], axis=1)

    def columns_to_parts(local):
        mine = own_and_other(local)
        return g.exchange_a(mine).reshape(A * 2 * rows_own, mine.shape[-1])

    qkv_local = jnp.concatenate(
        [
            w_query.reshape(rows_own, A, 2, q_cols),
            key_weight.reshape(rows_own, A, 2, HEAD_SIZE),
            value_weight.reshape(rows_own, A, 2, HEAD_SIZE),
        ],
        axis=-1,
    )
    x_own = permuted(tokens[0])
    x_parts = g.ring_a(x_own)
    qkv_own = g.spread(columns_to_parts(qkv_local), True)
    qkv_other = [g.swap(piece) for piece in qkv_own]

    packed = jnp.concatenate([attn_gain, mlp_gain, qk_gain.reshape(-1)])
    low, high = g.by_core(packed, g.swap(packed))
    packed = jnp.stack([low, high])
    packed = jnp.stack(g.spread(packed, True))
    packed = g.exchange_a(jnp.broadcast_to(packed[None], (A,) + packed.shape))
    packed = jnp.transpose(packed, (1, 0, 2, 3)).astype(f32)
    first_gain = packed[..., :rows_own].reshape(width)
    second_gain = packed[..., rows_own : 2 * rows_own].reshape(width)
    small = packed[..., 2 * rows_own :].reshape(R, Y, A, 2, 2, -1)
    small = jnp.stack([small[(b - i) % R] for i in range(R)])
    small = jnp.stack([small[:, (y - j) % Y] for j in range(Y)], axis=1)
    small = jnp.transpose(small, (4, 2, 0, 1, 3, 5)).reshape(2, HEAD_SIZE)
    query_gain, key_gain = small[0], small[1]

    out_local = own_and_other(w_out.reshape(rows_own, A, 2, q_cols))
    out_local = jnp.transpose(out_local, (1, 0, 2)).reshape(2 * rows_own, A * q_cols)
    out_all = g.exchange_a(jnp.broadcast_to(out_local[None], (A,) + out_local.shape))
    out_own = g.spread(out_all.reshape(A * 2 * rows_own, A * q_cols), False)
    out_other = [g.swap(piece) for piece in out_own]
    gu_local = jnp.concatenate(
        [w_gate.reshape(rows_own, A, 2, ff_cols), w_up.reshape(rows_own, A, 2, ff_cols)], axis=-1
    )
    gu_own = g.spread(columns_to_parts(gu_local), True)
    gu_other = [g.swap(piece) for piece in gu_own]
    down_own = g.spread(columns_to_parts(w_down.reshape(rows_own, A, 2, ff_cols)), False)
    down_other = [g.swap(piece) for piece in down_own]

    order = block_pos[0]
    row_offsets = jnp.arange(token_rows, dtype=jnp.int32)

    def positions(shift):
        blocks = [order[((a - d) % A) * R + (b - shift) % R] for d in range(A)]
        return jnp.concatenate([block * token_rows + row_offsets for block in blocks])

    local_pos = positions(0)
    key_pos = jnp.concatenate([positions(i) for i in range(R)])
    exponent = jnp.arange(HEAD_SIZE // 2, dtype=f32) * (-2.0 / HEAD_SIZE)
    angles = local_pos.astype(f32)[:, None] * (rope_base**exponent)[None, :]
    cosine, sine = jnp.cos(angles), jnp.sin(angles)
    cosine3, sine3 = cosine[:, None, :], sine[:, None, :]

    x_group = jnp.concatenate(x_parts, axis=0)
    inputs = x_group.astype(f32)
    x_root = inv_rms(inputs)
    normed = (inputs * x_root * first_gain).astype(bf16)

    def project(left, weights):
        total = dot(cut(left, 0), weights[0])
        for i in range(1, pieces):
            total = total + dot(cut(left, i), weights[i])
        return total

    def heads_of(weights):
        made = project(normed, weights)
        q_pre = made[:, :q_cols].reshape(group_rows, GROUP, HEAD_SIZE)
        k_pre = made[:, q_cols : q_cols + HEAD_SIZE]
        value = made[:, q_cols + HEAD_SIZE :].astype(bf16)
        q_root, k_root = inv_rms(q_pre), inv_rms(k_pre)
        query = rotate(q_pre * q_root * query_gain, cosine3, sine3).astype(bf16)
        key = rotate(k_pre * k_root * key_gain, cosine, sine).astype(bf16)
        return q_pre, q_root, query, k_pre, k_root, key, value

    made = [heads_of(qkv_own), heads_of(qkv_other)]
    key_values = jnp.concatenate([made[0][5], made[0][6], made[1][5], made[1][6]], axis=1)
    key_values = jnp.concatenate(
        [key_values] + [g.move(key_values, b=i) for i in range(1, R)], axis=0
    )

    visible = local_pos[:, None] >= key_pos[None, :]

    def attend(h):
        query = made[h][2]
        key = key_values[:, 2 * h * HEAD_SIZE : (2 * h + 1) * HEAD_SIZE]
        value = key_values[:, (2 * h + 1) * HEAD_SIZE : (2 * h + 2) * HEAD_SIZE]
        scores = jnp.einsum("qgd,td->gqt", query, key, preferred_element_type=f32) * score_scale
        scores = jnp.where(visible, scores, -1e30)
        top = jnp.max(scores, axis=-1, keepdims=True)
        weights = jnp.exp(scores - top)
        totals = jnp.sum(weights, axis=-1, keepdims=True)
        log_total = top + jnp.log(totals)
        mixed = jnp.einsum("gqt,td->gqd", weights.astype(bf16), value, preferred_element_type=f32)
        return mixed / totals, log_total

    mixed = [attend(0), attend(1)]
    attended = jnp.concatenate(
        [jnp.transpose(m[0], (1, 0, 2)).reshape(group_rows, q_cols) for m in mixed], axis=1
    ).astype(bf16)
    attended = jnp.stack(
        [jnp.roll(got, d * token_rows, axis=0) for d, got in enumerate(g.ring_a(attended))]
    )
    attended = jnp.stack([attended[(a - part) % A] for part in range(A)])
    att_own = jnp.concatenate([attended[part, :, :q_cols] for part in range(A)], axis=1)
    att_other = jnp.concatenate([attended[part, :, q_cols:] for part in range(A)], axis=1)

    branch = jnp.concatenate(
        [dot_t(att_own, out_own[i]) + dot_t(att_other, out_other[i]) for i in range(pieces)], axis=1
    )
    middle = inputs + branch
    root2 = inv_rms(middle)
    normed2 = (middle * root2 * second_gain).astype(bf16)
    dout_own = permuted(grad_out[0])
    dout = jnp.concatenate(g.ring_a(dout_own), axis=0)

    def feed(weights):
        both = project(normed2, weights)
        return both[:, :ff_cols], both[:, ff_cols:]

    gates = [feed(gu_own), feed(gu_other)]
    inner = [(jax.nn.silu(gate) * up).astype(bf16) for gate, up in gates]
    d_inner = [project(dout, down_own), project(dout, down_other)]

    def gate_back(gate, up, d_in):
        s = jax.nn.sigmoid(gate)
        d_gate = d_in * up * s * (1.0 + gate * (1.0 - s))
        return jnp.concatenate([d_gate, d_in * gate * s], axis=1).astype(bf16)

    d_gu = [gate_back(*gates[h], d_inner[h]) for h in range(2)]
    d_normed2 = jnp.concatenate(
        [dot_t(d_gu[0], gu_own[i]) + dot_t(d_gu[1], gu_other[i]) for i in range(pieces)], axis=1
    )
    mlp_gain_grad = jnp.sum(d_normed2 * middle * root2, axis=0)
    e2 = g.sum_over_a(d_normed2, token_rows)
    grad_middle = dout_own.astype(f32) + norm_back(
        middle[:token_rows], root2[:token_rows], second_gain, e2
    )
    out_part = jnp.concatenate(
        [dot_t(inner[0], down_own[i]) + dot_t(inner[1], down_other[i]) for i in range(pieces)],
        axis=1,
    )
    result = restored((middle[:token_rows] + g.sum_over_a(out_part, token_rows)).astype(bf16))

    def weight_gradient(left, own, other, b_first):
        lefts = [cut(left, i) for i in range(pieces)]
        sent = [g.swap(dot_tn(part, other).astype(bf16)) for part in lefts]
        kept = [
            (dot_tn(part, own) + got.astype(f32)).astype(bf16) for part, got in zip(lefts, sent)
        ]
        total = g.collect(kept, b_first).astype(bf16)
        total = g.exchange_a(total.reshape(A, 2 * rows_own, -1)).reshape(A, 2, rows_own, -1)
        keep = lax.dynamic_index_in_dim(total, c, 1, keepdims=False)
        send = lax.dynamic_index_in_dim(total, 1 - c, 1, keepdims=False)
        low, high = g.by_core(keep, g.swap(send))
        whole = jnp.stack([low, high], axis=1)
        return jnp.transpose(whole, (2, 0, 1, 3)).astype(f32)

    gu_grad = weight_gradient(normed2, d_gu[0], d_gu[1], True)
    down_grad = weight_gradient(dout, inner[0], inner[1], False)

    d_branch = grad_middle.astype(bf16)

    def to_parts(array, cols):
        send = [
            lax.dynamic_slice_in_dim(array, ((a + d) % A) * cols, cols, axis=1) for d in range(A)
        ]
        return [send[0]] + [g.move(send[d], a=d) for d in range(1, A)]

    def out_back(i):
        return dot(cut(d_branch, i), out_own[i]), dot(cut(d_branch, i), out_other[i])

    d_att_own, d_att_other = out_back(0)
    for i in range(1, pieces):
        more_own, more_other = out_back(i)
        d_att_own, d_att_other = d_att_own + more_own, d_att_other + more_other
    d_att = jnp.concatenate(
        [
            d_att_own.reshape(token_rows, A, q_cols),
            d_att_other.reshape(token_rows, A, q_cols),
        ],
        axis=-1,
    ).astype(bf16)
    d_att = jnp.concatenate(to_parts(d_att.reshape(token_rows, A * 2 * q_cols), 2 * q_cols), axis=0)

    def attend_back(h):
        query = made[h][2]
        key = key_values[:, 2 * h * HEAD_SIZE : (2 * h + 1) * HEAD_SIZE]
        value = key_values[:, (2 * h + 1) * HEAD_SIZE : (2 * h + 2) * HEAD_SIZE]
        d_mixed = d_att[:, h * q_cols : (h + 1) * q_cols].reshape(group_rows, GROUP, HEAD_SIZE)
        o, log_total = mixed[h]
        delta = jnp.sum(jnp.transpose(d_mixed, (1, 0, 2)).astype(f32) * o, axis=-1, keepdims=True)
        scores = jnp.einsum("qgd,td->gqt", query, key, preferred_element_type=f32) * score_scale
        scores = jnp.where(visible, scores, -1e30)
        weights = jnp.exp(scores - log_total)
        d_weights = jnp.einsum("qgd,td->gqt", d_mixed, value, preferred_element_type=f32)
        d_scores = (weights * (d_weights - delta)).astype(bf16)
        d_query = jnp.einsum("gqt,td->qgd", d_scores, key, preferred_element_type=f32)
        d_key = jnp.einsum("gqt,qgd->td", d_scores, query, preferred_element_type=f32)
        d_value = jnp.einsum(
            "gqt,qgd->td", weights.astype(bf16), d_mixed, preferred_element_type=f32
        )
        return d_query * score_scale, d_key, d_value

    backs = [attend_back(0), attend_back(1)]
    d_kv = jnp.concatenate([backs[0][1], backs[0][2], backs[1][1], backs[1][2]], axis=1)
    d_kv_total = d_kv[:group_rows]
    for i in range(1, R):
        block = d_kv[i * group_rows : (i + 1) * group_rows].astype(bf16)
        d_kv_total = d_kv_total + g.move(block, b=-i).astype(f32)

    def projections_back(h):
        q_pre, q_root, _, k_pre, k_root, _, _ = made[h]
        e_q = unrotate(backs[h][0], cosine3, sine3)
        d_key = d_kv_total[:, 2 * h * HEAD_SIZE : (2 * h + 1) * HEAD_SIZE] * score_scale
        d_value = d_kv_total[:, (2 * h + 1) * HEAD_SIZE : (2 * h + 2) * HEAD_SIZE]
        e_k = unrotate(d_key, cosine, sine)
        d_q_pre = norm_back(q_pre, q_root, query_gain, e_q).reshape(group_rows, q_cols)
        d_k_pre = norm_back(k_pre, k_root, key_gain, e_k)
        gains = jnp.stack(
            [jnp.sum(e_q * q_pre * q_root, axis=(0, 1)), jnp.sum(e_k * k_pre * k_root, axis=0)]
        )
        return jnp.concatenate([d_q_pre, d_k_pre, d_value], axis=1).astype(bf16), gains

    d_qkv_own, gains_own = projections_back(0)
    d_qkv_other, gains_other = projections_back(1)
    d_normed = jnp.concatenate(
        [
            dot_t(d_qkv_own, qkv_own[i]) + dot_t(d_qkv_other, qkv_other[i])
            for i in range(pieces)
        ],
        axis=1,
    )
    attn_gain_grad = jnp.sum(d_normed * inputs * x_root, axis=0)
    e1 = g.sum_over_a(d_normed, token_rows)
    grad_input = grad_middle + norm_back(
        inputs[:token_rows], x_root[:token_rows], first_gain, e1
    )
    qkv_grad = weight_gradient(normed, d_qkv_own, d_qkv_other, True)

    att_low, att_high = g.by_core(att_own, att_other)
    att_heads = jnp.stack(
        [att_low.reshape(group_rows, A, q_cols), att_high.reshape(group_rows, A, q_cols)], axis=2
    ).reshape(group_rows, A * 2 * q_cols)
    by_part = jnp.transpose(
        d_branch.reshape(token_rows, pieces, A, 2 * rows_own), (0, 2, 1, 3)
    ).reshape(token_rows, width)
    rows_of_part = jnp.concatenate(to_parts(by_part, pieces * 2 * rows_own), axis=0)
    out_grad = dot_tn(rows_of_part, att_heads).reshape(pieces, 2, rows_own, -1)
    keep = lax.dynamic_index_in_dim(out_grad, c, 1, keepdims=False)
    send = lax.dynamic_index_in_dim(out_grad, 1 - c, 1, keepdims=False).astype(bf16)
    out_grad = keep + g.swap(send).astype(f32)
    grad_wo = g.collect([out_grad[i] for i in range(pieces)], False)

    small = (gains_own + gains_other).reshape(2, A, R, Y, 2, -1)
    small = jnp.transpose(small, (2, 3, 1, 4, 0, 5))
    small = jnp.stack([small[(b - i) % R] for i in range(R)])
    small = jnp.stack([small[:, (y - j) % Y] for j in range(Y)], axis=1)
    small = small.reshape(pieces, A, 2, -1)
    sums = jnp.concatenate(
        [
            attn_gain_grad.reshape(pieces, A, 2, rows_own),
            mlp_gain_grad.reshape(pieces, A, 2, rows_own),
            small,
        ],
        axis=-1,
    )
    keep = lax.dynamic_index_in_dim(sums, c, 2, keepdims=False)
    send = lax.dynamic_index_in_dim(sums, 1 - c, 2, keepdims=False)
    sums = keep + g.swap(send)
    sums = g.collect([sums[i] for i in range(pieces)], True, wide=True)
    sums = jnp.sum(g.exchange_a(sums), axis=0)

    gate_up = gu_grad.reshape(rows_own, 2 * A, 2, ff_cols)
    return (
        result[None],
        restored(grad_input)[None],
        qkv_grad[..., :q_cols].reshape(rows_own, -1),
        qkv_grad[..., q_cols : q_cols + HEAD_SIZE].reshape(rows_own, -1),
        qkv_grad[..., q_cols + HEAD_SIZE :].reshape(rows_own, -1),
        grad_wo,
        gate_up[:, :, 0].reshape(rows_own, -1),
        gate_up[:, :, 1].reshape(rows_own, -1),
        down_grad.reshape(rows_own, -1),
        sums[:rows_own],
        sums[rows_own : 2 * rows_own],
        sums[2 * rows_own :].reshape(2, -1),
    )


def solution(mesh):
    placed = (
        P("fsdp", "seq", None),
        P("fsdp", None),
        P(("seq", "fsdp"), None),
        P(("seq", "fsdp"), None),
        P(("seq", "fsdp"), None),
        P(("seq", "fsdp"), None),
        P(("seq", "fsdp"), None),
        P(("seq", "fsdp"), None),
        P(("seq", "fsdp"), None),
        P(("seq", "fsdp")),
        P(("seq", "fsdp")),
        P(None, ("seq", "fsdp")),
        P("fsdp", "seq", None),
    )
    return jax.shard_map(
        on_device,
        mesh=mesh,
        in_specs=placed,
        out_specs=(
            P("fsdp", "seq", None),
            P("fsdp", "seq", None),
            P(("seq", "fsdp"), None),
            P(("seq", "fsdp"), None),
            P(("seq", "fsdp"), None),
            P(("seq", "fsdp"), None),
            P(("seq", "fsdp"), None),
            P(("seq", "fsdp"), None),
            P(("seq", "fsdp"), None),
            P(("seq", "fsdp")),
            P(("seq", "fsdp")),
            P(None, ("seq", "fsdp")),
        ),
        check_vma=False,
    )
```

```python
import jax
import jax.numpy as jnp
import numpy as np
from jax import lax
from jax.experimental import pallas as pl
from jax.experimental.pallas import tpu as pltpu
from jax.sharding import PartitionSpec as P

QUERY_HEADS = 16
KEY_VALUE_HEADS = 8
HEAD_SIZE = 128
FF = 6144

rope_base = 1000000.0
norm_eps = 1e-06
BOTH = ("seq", "fsdp")
bf16 = jnp.bfloat16
f32 = jnp.float32

PARTS = KEY_VALUE_HEADS // 2
GROUP = QUERY_HEADS // KEY_VALUE_HEADS


LANES = 128
EXTRA = 16
VMEM_BYTES = 48 * 1024 * 1024
ALL_VMEM_BYTES = 60 * 1024 * 1024


def dot(left, right):
    return jnp.dot(left, right, preferred_element_type=f32)


def dot_t(left, right):
    return lax.dot_general(left, right, (((1,), (1,)), ((), ())), preferred_element_type=f32)


def dot_tn(left, right):
    return lax.dot_general(left, right, (((0,), (0,)), ((), ())), preferred_element_type=f32)


def inv_rms(tensor):
    return lax.rsqrt(jnp.mean(tensor * tensor, axis=-1, keepdims=True) + norm_eps)


def norm_back(tensor, root, gain, incoming):
    scaled = gain * incoming
    return root * scaled - tensor * (root * root * root) * jnp.mean(
        scaled * tensor, axis=-1, keepdims=True
    )


def halves(tensor):
    half_width = tensor.shape[-1] // 2
    return tensor[..., :half_width], tensor[..., half_width:]


def rotate(tensor, cosine, sine):
    front, back = halves(tensor)
    return jnp.concatenate([front * cosine - back * sine, back * cosine + front * sine], axis=-1)


def unrotate(tensor, cosine, sine):
    front, back = halves(tensor)
    return jnp.concatenate([front * cosine + back * sine, back * cosine - front * sine], axis=-1)


class Grid:
    def __init__(self):
        self.fsdp = lax.axis_size("fsdp")
        self.A = PARTS
        self.R = lax.axis_size("seq") // self.A
        self.Y = self.fsdp // 2
        s, f = lax.axis_index("seq"), lax.axis_index("fsdp")
        self.a, self.b = s // self.R, s % self.R
        self.y, self.c = f // 2, f % 2
        self.places = [
            (a, b, y, c)
            for a in range(self.A)
            for b in range(self.R)
            for y in range(self.Y)
            for c in range(2)
        ]

    def at(self, a, b, y, c):
        return (a * self.R + b % self.R) * self.fsdp + (y % self.Y) * 2 + c % 2

    def groups(self, along):
        found = {}
        for place in self.places:
            fixed = tuple(v for v, name in zip(place, "abyc") if name not in along)
            found.setdefault(fixed, []).append(self.at(*place))
        return list(found.values())

    def move(self, array, a=0, b=0, y=0, c=0):
        route = [
            (self.at(*p), self.at(p[0] ^ a, p[1] + b, p[2] + y, p[3] + c)) for p in self.places
        ]
        return lax.ppermute(array, BOTH, route)

    def swap(self, array):
        return self.move(array, c=1)

    def exchange_a(self, array):
        return lax.all_to_all(array, BOTH, 0, 0, axis_index_groups=self.groups("a"), tiled=True)

    def gather_by(self, array):
        return lax.all_gather(array, BOTH, axis_index_groups=self.groups("by"), axis=0, tiled=True)

    def scatter(self, along, array):
        return lax.psum_scatter(
            array, BOTH, axis_index_groups=self.groups(along), scatter_dimension=0, tiled=True
        )

    def deal_a(self, blocks):
        return [blocks[0]] + [self.move(blocks[d], a=d) for d in range(1, self.A)]

    def gather_a(self, array):
        return self.deal_a([array] * self.A)

    def ahead(self, array):
        return [
            lax.dynamic_index_in_dim(array, self.a ^ d, 0, keepdims=False) for d in range(self.A)
        ]

    def in_place(self, blocks):
        held = jnp.stack(blocks)
        return jnp.stack(
            [
                lax.dynamic_index_in_dim(held, self.a ^ part, 0, keepdims=False)
                for part in range(self.A)
            ]
        )

    def by_core(self, first, second):
        return (
            jnp.where(self.c == 0, first, second),
            jnp.where(self.c == 0, second, first),
        )

    def pairs(self):
        return [(i, j) for i in range(self.R) for j in range(self.Y)]

    def spread(self, piece):
        return [piece] + [self.move(piece, b=i, y=j) for i, j in self.pairs()[1:]]

    def mine_first(self, pieces):
        return [
            lax.dynamic_index_in_dim(
                pieces, (self.b - i) % self.R * self.Y + (self.y - j) % self.Y, 0, False
            )
            for i, j in self.pairs()
        ]

    def collect(self, pieces, *late):
        held = self.mine_first(pieces)
        got = [self.move(part, b=-i, y=-j) for part, (i, j) in zip(held[1:], self.pairs()[1:])]
        got = after(got, *late) if late else got
        return added(held[0], got)

    def to_rows_owner(self, partial):
        got = self.exchange_a(partial.reshape(self.A, -1, partial.shape[1]))
        return added(got[0], list(got[1:]))


def added(first, rest):
    total = first.astype(f32)
    for part in rest:
        total = total + part.astype(f32)
    return total


def whole_call(body, scalars, ins, outs):
    return pl.pallas_call(
        body,
        grid_spec=pltpu.PrefetchScalarGridSpec(
            num_scalar_prefetch=1,
            grid=(1,),
            in_specs=[pl.BlockSpec(v.shape, lambda i, s, n=v.ndim: (0,) * n) for v in ins],
            out_specs=[pl.BlockSpec(v.shape, lambda i, s, n=len(v.shape): (0,) * n) for v in outs],
        ),
        out_shape=outs,
        compiler_params=pltpu.CompilerParams(vmem_limit_bytes=VMEM_BYTES),
    )(scalars, *ins)


def like(shape, kind=bf16):
    return jax.ShapeDtypeStruct(shape, kind)


def at_multiple(number, size):
    return pl.ds(pl.multiple_of(number * size, size), size)


def reorder(arrays, source):
    count = len(arrays)

    def body(_, *refs):
        for i, at in enumerate(source):
            for src, dst in zip(refs[:count], refs[count:]):
                dst[:, i * LANES : (i + 1) * LANES] = src[:, at * LANES : (at + 1) * LANES]

    return whole_call(
        body, jnp.zeros((1,), jnp.int32), arrays, [like(v.shape, v.dtype) for v in arrays]
    )


def cut_columns(groups, spot, parts):
    flat = [a for group in groups for a in group]
    rows = flat[0].shape[0]
    widths = [a.shape[1] // (2 * parts) for a in flat]
    group_widths = [sum(a.shape[1] // (2 * parts) for a in group) for group in groups]

    def body(spot_ref, *refs):
        ins, outs = refs[: len(flat)], refs[len(flat) :]
        for half in range(2):
            core = spot_ref[0] if half == 0 else 1 - spot_ref[0]
            at = 0
            for k, group in enumerate(groups):
                start = 0
                for _ in group:
                    n = widths[at]
                    outs[2 * k + half][0, :, start : start + n] = ins[at][:, at_multiple(core, n)]
                    start += n
                    at += 1

    out_specs, out_shape = [], []
    for n in group_widths:
        for _ in range(2):
            out_specs.append(pl.BlockSpec((1, rows, n), lambda i, spot: (i, 0, 0)))
            out_shape.append(like((parts, rows, n)))
    made = pl.pallas_call(
        body,
        grid_spec=pltpu.PrefetchScalarGridSpec(
            num_scalar_prefetch=1,
            grid=(parts,),
            in_specs=[pl.BlockSpec((rows, 2 * n), lambda i, spot: (0, i)) for n in widths],
            out_specs=out_specs,
        ),
        out_shape=out_shape,
        compiler_params=pltpu.CompilerParams(vmem_limit_bytes=ALL_VMEM_BYTES),
    )(spot, *flat)
    return [(made[2 * k], made[2 * k + 1]) for k in range(len(groups))]


def merge_with_extra(keep, got, extras, spot):
    parts, rows, n = keep.shape
    more = extras[0].shape[0]

    def body(spot_ref, keep_ref, got_ref, own_ref, other_ref, out):
        here, there = spot_ref[0], 1 - spot_ref[0]
        for part in range(parts):
            out[part, at_multiple(here, rows), :] = keep_ref[part]
            out[part, at_multiple(there, rows), :] = got_ref[part]
            for core, ref in ((here, own_ref), (there, other_ref)):
                where = pl.ds(pl.multiple_of(2 * rows + core * more, more), more)
                out[part, where, :] = ref[...]

    return whole_call(
        body, spot, [keep, got, *extras], [like((parts, 2 * (rows + more), n))]
    )[0]


def merge_rows(keep, got, spot, widths):
    parts, rows, _ = keep.shape

    def body(spot_ref, keep_ref, got_ref, *outs):
        for part in range(parts):
            for core, ref in ((spot_ref[0], keep_ref), (1 - spot_ref[0], got_ref)):
                start = 0
                for n, out in zip(widths, outs):
                    out[part, at_multiple(core, rows), :] = ref[part, :, start : start + n]
                    start += n

    return whole_call(body, spot, [keep, got], [like((parts, 2 * rows, n)) for n in widths])


def stack_parts(blocks, spot):
    parts = len(blocks)
    rows, n = blocks[0].shape

    def body(spot_ref, *refs):
        for d in range(parts):
            refs[parts][at_multiple(spot_ref[1] ^ d, rows), :] = refs[d][...]

    return whole_call(body, spot, blocks, [like((parts * rows, n))])[0]


def reorder_rows(array, source):
    rows = array.shape[0] // len(source)

    def body(_, src, dst):
        for i, at in enumerate(source):
            dst[i * rows : (i + 1) * rows, :] = src[at * rows : (at + 1) * rows, :]

    return whole_call(body, jnp.zeros((1,), jnp.int32), [array], [like(array.shape)])[0]


def stack_with_extra(blocks, where, parts, rows, more):
    n = blocks[0].shape[1]

    def body(where_ref, *refs):
        for k in range(len(blocks)):
            for part in range(parts):
                start = part * (rows + more)
                place = part * len(blocks) + where_ref[k]
                refs[-2][at_multiple(place, rows), :] = refs[k][start : start + rows, :]
                refs[-1][at_multiple(place, more), :] = refs[k][start + rows : start + rows + more, :]

    total = len(blocks) * parts
    return whole_call(body, where, blocks, [like((total * rows, n)), like((total * more, n))])


def gather_heads(blocks, spot, half):
    parts = len(blocks)
    tokens = blocks[0].shape[0]

    def body(spot_ref, *refs):
        for d in range(parts):
            for k, core in enumerate((spot_ref[0], 1 - spot_ref[0])):
                where = at_multiple(2 * (spot_ref[1] ^ d) + core, half)
                refs[-1][:, where] = refs[d][:, k * half : (k + 1) * half]

    return whole_call(body, spot, blocks, [like((tokens, 2 * parts * half))])[0]


def column_blocks(arrays, parts):
    rows = arrays[0].shape[0]
    widths = [array.shape[1] // parts for array in arrays]

    def body(_, *refs):
        for part in range(parts):
            start = 0
            for n, src in zip(widths, refs):
                refs[-1][part, :, start : start + n] = src[:, part * n : (part + 1) * n]
                start += n

    return whole_call(
        body, jnp.zeros((1,), jnp.int32), arrays, [like((parts, rows, sum(widths)))]
    )[0]


def join_columns(keep, got, spot, widths):
    parts, rows, total = keep.shape

    def body(spot_ref, keep_ref, got_ref, *outs):
        mine = pl.program_id(1) == spot_ref[0]
        start = 0
        for n, out in zip(widths, outs):
            part = slice(start, start + n)
            out[...] = jnp.where(mine, keep_ref[0, :, part], got_ref[0, :, part]).astype(f32)
            start += n

    block = pl.BlockSpec((1, rows, total), lambda i, h, spot: (i, 0, 0))
    return pl.pallas_call(
        body,
        grid_spec=pltpu.PrefetchScalarGridSpec(
            num_scalar_prefetch=1,
            grid=(parts, 2),
            in_specs=[block, block],
            out_specs=[pl.BlockSpec((rows, n), lambda i, h, spot: (0, 2 * i + h)) for n in widths],
        ),
        out_shape=[like((rows, 2 * parts * n), f32) for n in widths],
        compiler_params=pltpu.CompilerParams(vmem_limit_bytes=VMEM_BYTES),
    )(spot, keep, got)


def token_products(groups, orders):
    counts = [len(lefts) for lefts, _ in groups]
    tokens, width = groups[0][0][0].shape
    widths = [rights[0].shape[1] for _, rights in groups]
    blocks = len(orders[0])
    unit = width // blocks
    steps = min(4, blocks)
    per_step = blocks // steps

    def body(order_ref, *refs):
        for k in range(per_step):
            at, start = 0, 0
            for m, (count, n) in enumerate(zip(counts, widths)):
                place = order_ref[m * blocks + pl.program_id(0) * per_step + k]
                where = at_multiple(place, unit)
                total = dot_tn(refs[at][:, where], refs[at + count][...])
                for i in range(1, count):
                    total = total + dot_tn(refs[at + i][:, where], refs[at + count + i][...])
                refs[-1][k * unit : (k + 1) * unit, start : start + n] = total.astype(bf16)
                at += 2 * count
                start += n

    flat = [v for lefts, rights in groups for v in (*lefts, *rights)]
    return pl.pallas_call(
        body,
        grid_spec=pltpu.PrefetchScalarGridSpec(
            num_scalar_prefetch=1,
            grid=(steps,),
            in_specs=[pl.BlockSpec(v.shape, lambda i, s: (0, 0)) for v in flat],
            out_specs=pl.BlockSpec((per_step * unit, sum(widths)), lambda i, s: (i, 0)),
        ),
        out_shape=like((width, sum(widths))),
        compiler_params=pltpu.CompilerParams(vmem_limit_bytes=VMEM_BYTES),
    )(jnp.asarray(np.concatenate(orders), jnp.int32), *flat)


def product_t(left, right, rows, add=None):
    tokens, n = left.shape
    width = right.shape[0]

    def body(left_ref, right_ref, *refs):
        made = dot_t(left_ref[...], right_ref[...])
        if add is not None:
            made = made + refs[0][...].astype(f32)
        refs[-1][...] = made.astype(refs[-1].dtype)

    ins = [left, right] + ([] if add is None else [add])
    block = pl.BlockSpec((tokens, rows), lambda i: (0, i))
    return pl.pallas_call(
        body,
        grid=(width // rows,),
        in_specs=[
            pl.BlockSpec((tokens, n), lambda i: (0, 0)),
            pl.BlockSpec((rows, n), lambda i: (i, 0)),
        ]
        + ([] if add is None else [block]),
        out_specs=block,
        out_shape=like((tokens, width)),
        compiler_params=pltpu.CompilerParams(vmem_limit_bytes=VMEM_BYTES),
    )(*ins)


def after(values, *others):
    return list(lax.optimization_barrier(tuple(values) + others))[: len(values)]


def on_device(
    tokens,
    block_pos,
    w_query,
    key_weight,
    value_weight,
    w_out,
    w_gate,
    w_up,
    w_down,
    attn_gain,
    mlp_gain,
    qk_gain,
    grad_out,
):
    g = Grid()
    A, R, Y = g.A, g.R, g.Y
    a, b, y, c = g.a, g.b, g.y, g.c
    pieces = R * Y
    rows_own = w_query.shape[0]
    width = tokens.shape[2]
    piece_width = width // pieces
    token_rows = tokens.shape[1]
    group_rows = A * token_rows
    score_scale = HEAD_SIZE ** (-0.5)
    q_cols = GROUP * HEAD_SIZE
    qkv_cols = q_cols + 2 * HEAD_SIZE
    ff_cols = FF // (2 * A)
    spot = jnp.stack([c, a]).astype(jnp.int32)

    unit = 2 * rows_own

    def permute(arrays, back):
        cuts = (R * Y, A, unit) if back else (A, R * Y, unit)
        columns = np.arange(width).reshape(cuts).transpose(1, 0, 2).reshape(-1)
        if unit % LANES == 0:
            return reorder(arrays, (columns[::LANES] // LANES).tolist())
        return [jnp.take(array, columns, axis=1) for array in arrays]

    places = jnp.stack(
        [(b - i) % R * Y + (y - j) % Y for i, j in g.pairs()]
    ).astype(jnp.int32)

    x_own, dout_own = tokens[0], grad_out[0]
    x_parts = g.gather_a(x_own)
    out_w = lax.all_gather(w_out, BOTH, axis=0, tiled=True)
    cuts = cut_columns(
        [[w_query, key_weight, value_weight], [w_gate, w_up, w_down]], spot, A
    )
    packed = jnp.concatenate([attn_gain, mlp_gain, qk_gain.reshape(-1)])
    packed = jnp.stack(
        [jnp.pad(v, (0, qkv_cols - v.shape[0])) for v in (packed, block_pos[0].astype(bf16))]
    )
    packed = jnp.pad(packed, ((0, EXTRA - 2), (0, 0)))
    sent = jnp.concatenate([cuts[0][1].reshape(A * rows_own, qkv_cols), packed])
    got = g.swap(sent)
    other_packed = got[A * rows_own :]
    qkv_local = merge_with_extra(
        cuts[0][0],
        got[: A * rows_own].reshape(A, rows_own, qkv_cols),
        [packed, other_packed],
        spot,
    )
    qkv_piece = g.exchange_a(qkv_local).reshape(-1, qkv_cols)
    qkv_w, extras = stack_with_extra(g.spread(qkv_piece), places, A, unit, 2 * EXTRA)
    packed = extras.reshape(2 * A * pieces, EXTRA, qkv_cols)[:, 0].astype(f32)
    first_gain = packed[..., :rows_own].reshape(width)
    second_gain = packed[..., rows_own : 2 * rows_own].reshape(width)
    small = packed[..., 2 * rows_own : 2 * rows_own + 2 * (HEAD_SIZE // (2 * pieces * A))]
    small = jnp.transpose(small.reshape(2 * A * pieces, 2, -1), (1, 0, 2)).reshape(2, HEAD_SIZE)
    query_gain, key_gain = small[0], small[1]

    gu_local, down_local = merge_rows(cuts[1][0], g.swap(cuts[1][1]), spot, [2 * ff_cols, ff_cols])
    (gu_local,) = after([gu_local], qkv_w, *x_parts)
    gu_piece = g.exchange_a(gu_local).reshape(A * unit, 2 * ff_cols)
    (down_local,) = after([down_local], gu_piece)
    down_piece = g.exchange_a(down_local).reshape(A * unit, ff_cols)

    blocks_seen = block_pos.shape[1]
    orders = [block_pos[0], other_packed[1, :blocks_seen].astype(jnp.int32)]
    row_offsets = jnp.arange(token_rows, dtype=jnp.int32)

    def positions(order, shift):
        blocks = [order[part * R + (b - shift) % R] for part in range(A)]
        return jnp.concatenate([block * token_rows + row_offsets for block in blocks])

    local_pos = [positions(order, 0) for order in orders]
    key_pos = [jnp.concatenate([positions(order, i) for i in range(R)]) for order in orders]
    exponent = jnp.arange(HEAD_SIZE // 2, dtype=f32) * (-2.0 / HEAD_SIZE)
    angles = jnp.concatenate(local_pos).astype(f32)[:, None] * (rope_base**exponent)[None, :]
    cosine, sine = jnp.cos(angles), jnp.sin(angles)
    cosine3, sine3 = cosine[:, None, :], sine[:, None, :]

    x_group = stack_parts(x_parts, spot)
    inputs = x_group.astype(f32)
    x_root = inv_rms(inputs)
    normed_own = (inputs * x_root * first_gain).astype(bf16)
    normed = [normed_own, g.swap(normed_own)]
    made = jnp.concatenate([dot(part, qkv_w) for part in normed], axis=0)
    gu_by = g.gather_by(after([gu_piece], out_w, made)[0])
    down_w = g.gather_by(down_piece)
    q_pre = made[:, :q_cols].reshape(2 * group_rows, GROUP, HEAD_SIZE)
    k_pre = made[:, q_cols : q_cols + HEAD_SIZE]
    value = made[:, q_cols + HEAD_SIZE :].astype(bf16)
    q_root, k_root = inv_rms(q_pre), inv_rms(k_pre)
    query = rotate(q_pre * q_root * query_gain, cosine3, sine3).astype(bf16)
    key = rotate(k_pre * k_root * key_gain, cosine, sine).astype(bf16)
    key_values = jnp.concatenate([key, value], axis=1)
    key_values = [key_values] + [g.move(key_values, b=i) for i in range(1, R)]

    def of_sequence(array, n):
        return array[n * group_rows : (n + 1) * group_rows]

    keys = [
        jnp.concatenate([of_sequence(kv, n)[:, :HEAD_SIZE] for kv in key_values]) for n in range(2)
    ]
    values = [
        jnp.concatenate([of_sequence(kv, n)[:, HEAD_SIZE:] for kv in key_values]) for n in range(2)
    ]

    visible = [local_pos[n][:, None] >= key_pos[n][None, :] for n in range(2)]

    def attend(n):
        scores = jnp.einsum(
            "qgd,td->gqt", of_sequence(query, n), keys[n], preferred_element_type=f32
        )
        scores = jnp.where(visible[n], scores * score_scale, -1e30)
        top = jnp.max(scores, axis=-1, keepdims=True)
        weights = jnp.exp(scores - top)
        totals = jnp.sum(weights, axis=-1, keepdims=True)
        log_total = top + jnp.log(totals)
        mixed = jnp.einsum(
            "gqt,td->gqd", weights.astype(bf16), values[n], preferred_element_type=f32
        )
        return mixed / totals, log_total

    def flat(heads):
        return jnp.transpose(heads, (1, 0, 2)).reshape(group_rows, q_cols).astype(bf16)

    mixed_other = attend(1)
    got = g.swap(flat(mixed_other[0]))
    mixed = [attend(0), mixed_other]
    attended = jnp.concatenate([flat(mixed[0][0]), got], axis=1)
    (attended,) = after([attended], down_piece)
    att_parts = g.gather_a(attended)
    att_heads = gather_heads(att_parts, spot, q_cols)

    (dout_by,) = permute(after([dout_own], att_parts[-1]), False)
    dout_parts = g.gather_a(dout_by)
    middle = inputs + dot_t(att_heads, out_w)
    root2 = inv_rms(middle)
    normed2_own = (middle * root2 * second_gain).astype(bf16)
    normed2 = [normed2_own, g.swap(normed2_own)]
    gu_w = reorder_rows(gu_by, np.arange(R * Y * A).reshape(R * Y, A).T.reshape(-1).tolist())
    both = [dot(part, gu_w) for part in normed2]
    dout_group = stack_parts(after(dout_parts, both[0]), spot)
    dout = [dout_group, g.swap(dout_group)]
    d_inner = [dot(part, down_w) for part in dout]

    def feed(n):
        gate, up = both[n][:, :ff_cols], both[n][:, ff_cols:]
        s = jax.nn.sigmoid(gate)
        act = gate * s
        d_gate = d_inner[n] * up * s * (1.0 + gate * (1.0 - s))
        return (
            (act * up).astype(bf16),
            jnp.concatenate([d_gate, d_inner[n] * act], axis=1).astype(bf16),
        )

    fed = [feed(0), feed(1)]
    inner, d_gu = [f[0] for f in fed], [f[1] for f in fed]

    def of_both(parts, weight):
        got = g.swap(product_t(parts[1], weight, 512))
        return product_t(parts[0], weight, 512, got)

    def own_rows(array):
        return lax.dynamic_slice_in_dim(array, a * token_rows, token_rows, axis=0)

    d_normed2 = of_both(d_gu, gu_w)
    mlp_gain_grad = jnp.sum(d_normed2 * middle * root2, axis=0)
    e2 = g.to_rows_owner(d_normed2)
    middle_own = own_rows(middle)
    grad_middle = dout_own.astype(f32) + norm_back(middle_own, own_rows(root2), second_gain, e2)

    by_order = np.arange(R * A * Y).reshape(A, R * Y).T.reshape(-1)

    def over_tokens(*groups):
        if unit % LANES == 0:
            orders = [by_order if natural else np.arange(R * A * Y) for _, _, natural in groups]
            return token_products([group[:2] for group in groups], orders)
        made = []
        for lefts, rights, natural in groups:
            total = dot_tn(lefts[0], rights[0]) + dot_tn(lefts[1], rights[1])
            total = total.reshape(R * A * Y, unit, -1)
            made.append(jnp.take(total, by_order, axis=0) if natural else total)
        return jnp.concatenate(made, axis=-1).reshape(width, -1).astype(bf16)

    def to_owner(dealt, widths):
        keep = lax.dynamic_index_in_dim(dealt, c, 1, keepdims=False)
        send = lax.dynamic_index_in_dim(dealt, 1 - c, 1, keepdims=False)
        return join_columns(keep, g.swap(send), spot, widths)

    def part_rows(total):
        return total.reshape(A, unit, -1)

    def core_rows(dealt):
        return dealt.reshape(A, 2, rows_own, -1)

    mlp_grad = over_tokens((after(normed2, d_normed2), d_gu, True), (dout, inner, False))
    mlp_total = g.scatter("by", mlp_grad)
    out_part = of_both(after(inner, mlp_grad), down_w)

    d_branch = grad_middle.astype(bf16)
    d_att = dot(d_branch, out_w).astype(bf16)
    if pieces * unit % LANES == 0:
        dealt = column_blocks([d_att, d_branch], A)
    else:
        dealt = jnp.concatenate([d_att.reshape(token_rows, A, -1), d_branch.reshape(token_rows, A, -1)], -1)
        dealt = jnp.swapaxes(dealt, 0, 1)
    dealt = g.exchange_a(dealt).reshape(group_rows, -1)
    d_att, rows_of_part = dealt[:, : 2 * q_cols], dealt[:, 2 * q_cols :]
    (out_part,) = after([out_part], d_att)
    out_mine = g.scatter("a", out_part)
    mlp_dealt = g.exchange_a(after([part_rows(mlp_total)], d_att)[0])
    mine_half, other_half = g.by_core(d_att[:, :q_cols], d_att[:, q_cols:])
    d_att = [mine_half, g.swap(other_half)]

    def attend_back(n):
        d_mixed = d_att[n].reshape(group_rows, GROUP, HEAD_SIZE)
        o, log_total = mixed[n]
        delta = jnp.sum(jnp.transpose(d_mixed, (1, 0, 2)).astype(f32) * o, axis=-1, keepdims=True)
        q = of_sequence(query, n)
        scores = jnp.einsum("qgd,td->gqt", q, keys[n], preferred_element_type=f32)
        scores = jnp.where(visible[n], scores * score_scale, -1e30)
        weights = jnp.exp(scores - log_total)
        d_weights = jnp.einsum("qgd,td->gqt", d_mixed, values[n], preferred_element_type=f32)
        d_scores = (weights * (d_weights - delta)).astype(bf16)
        d_query = jnp.einsum("gqt,td->qgd", d_scores, keys[n], preferred_element_type=f32)
        d_key = jnp.einsum("gqt,qgd->td", d_scores, q, preferred_element_type=f32)
        d_value = jnp.einsum(
            "gqt,qgd->td", weights.astype(bf16), d_mixed, preferred_element_type=f32
        )
        return d_query * score_scale, jnp.concatenate([d_key * score_scale, d_value], axis=1)

    backs = [attend_back(0), attend_back(1)]
    d_query = jnp.concatenate([back[0] for back in backs], axis=0)
    d_kv = jnp.concatenate([of_sequence(back[1], 0) for back in backs], axis=0)
    for i in range(1, R):
        block = jnp.concatenate([of_sequence(back[1], i) for back in backs], axis=0)
        d_kv = d_kv + g.move(block.astype(bf16), b=-i).astype(f32)
    e_q = unrotate(d_query, cosine3, sine3)
    e_k = unrotate(d_kv[:, :HEAD_SIZE], cosine, sine)
    d_q_pre = norm_back(q_pre, q_root, query_gain, e_q).reshape(2 * group_rows, q_cols)
    d_k_pre = norm_back(k_pre, k_root, key_gain, e_k)
    qk_gain_grad = jnp.stack(
        [jnp.sum(e_q * q_pre * q_root, axis=(0, 1)), jnp.sum(e_k * k_pre * k_root, axis=0)]
    )
    d_qkv = jnp.concatenate([d_q_pre, d_k_pre, d_kv[:, HEAD_SIZE:]], axis=1).astype(bf16)
    d_qkv = [of_sequence(d_qkv, 0), of_sequence(d_qkv, 1)]
    qkv_grad = over_tokens((normed, d_qkv, True))
    d_qkv = after(d_qkv, qkv_grad, mlp_dealt)
    d_normed = of_both(d_qkv, qkv_w)
    (out_sum,) = permute([out_mine.astype(f32)], True)
    result = (middle_own + out_sum).astype(bf16)
    qkv_total = g.scatter("by", qkv_grad)
    attn_gain_grad = jnp.sum(d_normed * inputs * x_root, axis=0)
    e1 = g.to_rows_owner(d_normed)
    grad_input = grad_middle + norm_back(
        x_own.astype(f32), inv_rms(x_own.astype(f32)), first_gain, e1
    )

    (qkv_total,) = after([qkv_total], e1)
    dealt = core_rows(g.exchange_a(part_rows(qkv_total)))
    grad_wq, grad_wk, grad_wv = to_owner(dealt, [q_cols, HEAD_SIZE, HEAD_SIZE])

    def by_first(array):
        return jnp.swapaxes(array, 0, 1).reshape(pieces, A, 2, -1)

    small = qk_gain_grad.reshape(2, A, pieces, 2, -1)
    small = jnp.transpose(small, (2, 1, 3, 0, 4)).reshape(pieces, A, 2, -1)
    sums = jnp.concatenate(
        [
            by_first(attn_gain_grad.reshape(A, pieces, 2, rows_own)),
            by_first(mlp_gain_grad.reshape(A, pieces, 2, rows_own)),
            small,
        ],
        axis=-1,
    )
    keep = lax.dynamic_index_in_dim(sums, c, 2, keepdims=False)
    send = lax.dynamic_index_in_dim(sums, 1 - c, 2, keepdims=False)
    sums = g.collect(keep + g.swap(send))
    sums = sum(g.deal_a(g.ahead(sums)))
    sums = [
        sums[:rows_own],
        sums[rows_own : 2 * rows_own],
        sums[2 * rows_own :].reshape(2, -1),
    ]

    (rows_of_part,) = after([rows_of_part], d_kv)
    grad_wo = g.scatter("byc", dot_tn(rows_of_part, att_heads).astype(bf16)).astype(f32)
    grad_wg, grad_wu, grad_wd = to_owner(core_rows(mlp_dealt), [ff_cols] * 3)
    return (
        result[None],
        grad_input[None],
        grad_wq,
        grad_wk,
        grad_wv,
        grad_wo,
        grad_wg,
        grad_wu,
        grad_wd,
        *sums,
    )


def solution(mesh):
    placed = (
        P("fsdp", "seq", None),
        P("fsdp", None),
        P(("seq", "fsdp"), None),
        P(("seq", "fsdp"), None),
        P(("seq", "fsdp"), None),
        P(("seq", "fsdp"), None),
        P(("seq", "fsdp"), None),
        P(("seq", "fsdp"), None),
        P(("seq", "fsdp"), None),
        P(("seq", "fsdp")),
        P(("seq", "fsdp")),
        P(None, ("seq", "fsdp")),
        P("fsdp", "seq", None),
    )
    return jax.shard_map(
        on_device,
        mesh=mesh,
        in_specs=placed,
        out_specs=(
            P("fsdp", "seq", None),
            P("fsdp", "seq", None),
            P(("seq", "fsdp"), None),
            P(("seq", "fsdp"), None),
            P(("seq", "fsdp"), None),
            P(("seq", "fsdp"), None),
            P(("seq", "fsdp"), None),
            P(("seq", "fsdp"), None),
            P(("seq", "fsdp"), None),
            P(("seq", "fsdp")),
            P(("seq", "fsdp")),
            P(None, ("seq", "fsdp")),
        ),
        check_vma=False,
    )
```

```python
import jax
import jax.numpy as jnp
import numpy as np
from jax import lax
from jax.experimental import pallas as pl
from jax.experimental.pallas import tpu as pltpu
from jax.sharding import PartitionSpec as P

QUERY_HEADS = 16
KEY_VALUE_HEADS = 8
HEAD_SIZE = 128
FF = 6144

rope_base = 1000000.0
norm_eps = 1e-06
BOTH = ("seq", "fsdp")
bf16 = jnp.bfloat16
f32 = jnp.float32

PARTS = KEY_VALUE_HEADS // 2
GROUP = QUERY_HEADS // KEY_VALUE_HEADS


LANES = 128
EXTRA = 16
VMEM_BYTES = 48 * 1024 * 1024
ALL_VMEM_BYTES = 60 * 1024 * 1024


def dot(left, right):
    return jnp.dot(left, right, preferred_element_type=f32)


def dot_t(left, right):
    return lax.dot_general(left, right, (((1,), (1,)), ((), ())), preferred_element_type=f32)


def dot_tn(left, right):
    return lax.dot_general(left, right, (((0,), (0,)), ((), ())), preferred_element_type=f32)


def inv_rms(tensor):
    return lax.rsqrt(jnp.mean(tensor * tensor, axis=-1, keepdims=True) + norm_eps)


def norm_back(tensor, root, gain, incoming):
    scaled = gain * incoming
    return root * scaled - tensor * (root * root * root) * jnp.mean(
        scaled * tensor, axis=-1, keepdims=True
    )


def halves(tensor):
    half_width = tensor.shape[-1] // 2
    return tensor[..., :half_width], tensor[..., half_width:]


def rotate(tensor, cosine, sine):
    front, back = halves(tensor)
    return jnp.concatenate([front * cosine - back * sine, back * cosine + front * sine], axis=-1)


def unrotate(tensor, cosine, sine):
    front, back = halves(tensor)
    return jnp.concatenate([front * cosine + back * sine, back * cosine - front * sine], axis=-1)


class Grid:
    def __init__(self):
        self.fsdp = lax.axis_size("fsdp")
        self.A = PARTS
        self.R = lax.axis_size("seq") // self.A
        self.Y = self.fsdp // 2
        s, f = lax.axis_index("seq"), lax.axis_index("fsdp")
        self.a, self.b = s // self.R, s % self.R
        self.y, self.c = f // 2, f % 2
        self.places = [
            (a, b, y, c)
            for a in range(self.A)
            for b in range(self.R)
            for y in range(self.Y)
            for c in range(2)
        ]

    def at(self, a, b, y, c):
        return (a * self.R + b % self.R) * self.fsdp + (y % self.Y) * 2 + c % 2

    def groups(self, along):
        found = {}
        for place in self.places:
            fixed = tuple(v for v, name in zip(place, "abyc") if name not in along)
            found.setdefault(fixed, []).append(self.at(*place))
        return list(found.values())

    def move(self, array, a=0, b=0, y=0, c=0):
        route = [
            (self.at(*p), self.at(p[0] ^ a, p[1] + b, p[2] + y, p[3] + c)) for p in self.places
        ]
        return lax.ppermute(array, BOTH, route)

    def swap(self, array):
        return self.move(array, c=1)

    def exchange_a(self, array):
        return lax.all_to_all(array, BOTH, 0, 0, axis_index_groups=self.groups("a"), tiled=True)

    def gather_by(self, array):
        return lax.all_gather(array, BOTH, axis_index_groups=self.groups("by"), axis=0, tiled=True)

    def scatter(self, along, array):
        return lax.psum_scatter(
            array, BOTH, axis_index_groups=self.groups(along), scatter_dimension=0, tiled=True
        )

    def deal_a(self, blocks):
        return [blocks[0]] + [self.move(blocks[d], a=d) for d in range(1, self.A)]

    def gather_a(self, array, own_first=True, then=()):
        held = {0: array}
        bit = self.A // 2
        while bit:
            own = self.move(array, a=bit)
            rest = [d for d in held if d]
            sent = [held[d] for d in rest]
            sent = after(sent, *((own,) if own_first else then)) if rest else sent
            held[bit] = own
            held.update({d | bit: self.move(v, a=bit) for d, v in zip(rest, sent)})
            bit //= 2
        return [held[d] for d in range(self.A)]

    def ahead(self, array):
        return [
            lax.dynamic_index_in_dim(array, self.a ^ d, 0, keepdims=False) for d in range(self.A)
        ]

    def in_place(self, blocks):
        held = jnp.stack(blocks)
        return jnp.stack(
            [
                lax.dynamic_index_in_dim(held, self.a ^ part, 0, keepdims=False)
                for part in range(self.A)
            ]
        )

    def by_core(self, first, second):
        return (
            jnp.where(self.c == 0, first, second),
            jnp.where(self.c == 0, second, first),
        )

    def pairs(self):
        return [(i, j) for i in range(self.R) for j in range(self.Y)]

    def spread(self, piece):
        return [piece] + [self.move(piece, b=i, y=j) for i, j in self.pairs()[1:]]

    def mine_first(self, pieces):
        return [
            lax.dynamic_index_in_dim(
                pieces, (self.b - i) % self.R * self.Y + (self.y - j) % self.Y, 0, False
            )
            for i, j in self.pairs()
        ]

    def collect(self, pieces, *late):
        held = self.mine_first(pieces)
        got = [self.move(part, b=-i, y=-j) for part, (i, j) in zip(held[1:], self.pairs()[1:])]
        got = after(got, *late) if late else got
        return added(held[0], got)

    def to_rows_owner(self, partial):
        got = self.exchange_a(partial.reshape(self.A, -1, partial.shape[1]))
        return added(got[0], list(got[1:]))


def added(first, rest):
    total = first.astype(f32)
    for part in rest:
        total = total + part.astype(f32)
    return total


def whole_call(body, scalars, ins, outs):
    return pl.pallas_call(
        body,
        grid_spec=pltpu.PrefetchScalarGridSpec(
            num_scalar_prefetch=1,
            grid=(1,),
            in_specs=[pl.BlockSpec(v.shape, lambda i, s, n=v.ndim: (0,) * n) for v in ins],
            out_specs=[pl.BlockSpec(v.shape, lambda i, s, n=len(v.shape): (0,) * n) for v in outs],
        ),
        out_shape=outs,
        compiler_params=pltpu.CompilerParams(vmem_limit_bytes=VMEM_BYTES),
    )(scalars, *ins)


def like(shape, kind=bf16):
    return jax.ShapeDtypeStruct(shape, kind)


def at_multiple(number, size):
    return pl.ds(pl.multiple_of(number * size, size), size)


def reorder(arrays, source):
    count = len(arrays)

    def body(_, *refs):
        for i, at in enumerate(source):
            for src, dst in zip(refs[:count], refs[count:]):
                dst[:, i * LANES : (i + 1) * LANES] = src[:, at * LANES : (at + 1) * LANES]

    return whole_call(
        body, jnp.zeros((1,), jnp.int32), arrays, [like(v.shape, v.dtype) for v in arrays]
    )


def cut_columns(groups, spot, parts):
    flat = [a for group in groups for a in group]
    rows = flat[0].shape[0]
    widths = [a.shape[1] // (2 * parts) for a in flat]
    group_widths = [sum(a.shape[1] // (2 * parts) for a in group) for group in groups]

    def body(spot_ref, *refs):
        ins, outs = refs[: len(flat)], refs[len(flat) :]
        for half in range(2):
            core = spot_ref[0] if half == 0 else 1 - spot_ref[0]
            at = 0
            for k, group in enumerate(groups):
                start = 0
                for _ in group:
                    n = widths[at]
                    outs[2 * k + half][0, :, start : start + n] = ins[at][:, at_multiple(core, n)]
                    start += n
                    at += 1

    out_specs, out_shape = [], []
    for n in group_widths:
        for _ in range(2):
            out_specs.append(pl.BlockSpec((1, rows, n), lambda i, spot: (i, 0, 0)))
            out_shape.append(like((parts, rows, n)))
    made = pl.pallas_call(
        body,
        grid_spec=pltpu.PrefetchScalarGridSpec(
            num_scalar_prefetch=1,
            grid=(parts,),
            in_specs=[pl.BlockSpec((rows, 2 * n), lambda i, spot: (0, i)) for n in widths],
            out_specs=out_specs,
        ),
        out_shape=out_shape,
        compiler_params=pltpu.CompilerParams(vmem_limit_bytes=ALL_VMEM_BYTES),
    )(spot, *flat)
    return [(made[2 * k], made[2 * k + 1]) for k in range(len(groups))]


def merge_with_extra(keep, got, extras, spot):
    parts, rows, n = keep.shape
    more = extras[0].shape[0]

    def body(spot_ref, keep_ref, got_ref, own_ref, other_ref, out):
        here, there = spot_ref[0], 1 - spot_ref[0]
        for part in range(parts):
            out[part, at_multiple(here, rows), :] = keep_ref[part]
            out[part, at_multiple(there, rows), :] = got_ref[part]
            for core, ref in ((here, own_ref), (there, other_ref)):
                where = pl.ds(pl.multiple_of(2 * rows + core * more, more), more)
                out[part, where, :] = ref[...]

    return whole_call(
        body, spot, [keep, got, *extras], [like((parts, 2 * (rows + more), n))]
    )[0]


def merge_rows(keep, got, spot, widths):
    parts, rows, _ = keep.shape

    def body(spot_ref, keep_ref, got_ref, *outs):
        for part in range(parts):
            for core, ref in ((spot_ref[0], keep_ref), (1 - spot_ref[0], got_ref)):
                start = 0
                for n, out in zip(widths, outs):
                    out[part, at_multiple(core, rows), :] = ref[part, :, start : start + n]
                    start += n

    return whole_call(body, spot, [keep, got], [like((parts, 2 * rows, n)) for n in widths])


def stack_parts(blocks, spot):
    parts = len(blocks)
    rows, n = blocks[0].shape

    def body(spot_ref, *refs):
        for d in range(parts):
            refs[parts][at_multiple(spot_ref[1] ^ d, rows), :] = refs[d][...]

    return whole_call(body, spot, blocks, [like((parts * rows, n))])[0]


def stack_with_extra(blocks, where, parts, rows, more):
    n = blocks[0].shape[1]

    def body(where_ref, *refs):
        for k in range(len(blocks)):
            for part in range(parts):
                start = part * (rows + more)
                place = part * len(blocks) + where_ref[k]
                refs[-2][at_multiple(place, rows), :] = refs[k][start : start + rows, :]
                refs[-1][at_multiple(place, more), :] = refs[k][start + rows : start + rows + more, :]

    total = len(blocks) * parts
    return whole_call(body, where, blocks, [like((total * rows, n)), like((total * more, n))])


def gather_heads(blocks, spot, half):
    parts = len(blocks)
    tokens = blocks[0].shape[0]

    def body(spot_ref, *refs):
        for d in range(parts):
            for k, core in enumerate((spot_ref[0], 1 - spot_ref[0])):
                where = at_multiple(2 * (spot_ref[1] ^ d) + core, half)
                refs[-1][:, where] = refs[d][:, k * half : (k + 1) * half]

    return whole_call(body, spot, blocks, [like((tokens, 2 * parts * half))])[0]


def column_blocks(arrays, parts):
    rows = arrays[0].shape[0]
    widths = [array.shape[1] // parts for array in arrays]

    def body(_, *refs):
        for part in range(parts):
            start = 0
            for n, src in zip(widths, refs):
                refs[-1][part, :, start : start + n] = src[:, part * n : (part + 1) * n]
                start += n

    return whole_call(
        body, jnp.zeros((1,), jnp.int32), arrays, [like((parts, rows, sum(widths)))]
    )[0]


def join_columns(keep, got, spot, widths):
    parts, rows, total = keep.shape

    def body(spot_ref, keep_ref, got_ref, *outs):
        mine = pl.program_id(1) == spot_ref[0]
        start = 0
        for n, out in zip(widths, outs):
            part = slice(start, start + n)
            out[...] = jnp.where(mine, keep_ref[0, :, part], got_ref[0, :, part]).astype(f32)
            start += n

    block = pl.BlockSpec((1, rows, total), lambda i, h, spot: (i, 0, 0))
    return pl.pallas_call(
        body,
        grid_spec=pltpu.PrefetchScalarGridSpec(
            num_scalar_prefetch=1,
            grid=(parts, 2),
            in_specs=[block, block],
            out_specs=[pl.BlockSpec((rows, n), lambda i, h, spot: (0, 2 * i + h)) for n in widths],
        ),
        out_shape=[like((rows, 2 * parts * n), f32) for n in widths],
        compiler_params=pltpu.CompilerParams(vmem_limit_bytes=VMEM_BYTES),
    )(spot, keep, got)


def token_products(groups, orders):
    counts = [len(lefts) for lefts, _ in groups]
    tokens, width = groups[0][0][0].shape
    widths = [rights[0].shape[1] for _, rights in groups]
    blocks = len(orders[0])
    unit = width // blocks
    steps = min(4, blocks)
    per_step = blocks // steps

    in_turn = [bool(np.array_equal(order, np.arange(blocks))) for order in orders]

    def body(order_ref, *refs):
        at, start = 0, 0
        for m, (count, n) in enumerate(zip(counts, widths)):
            first = pl.program_id(0) * per_step
            if in_turn[m]:
                places = [at_multiple(pl.program_id(0), per_step * unit)]
            else:
                places = [
                    at_multiple(order_ref[m * blocks + first + k], unit) for k in range(per_step)
                ]
            size = per_step * unit // len(places)
            for k, where in enumerate(places):
                total = dot_tn(refs[at][:, where], refs[at + count][...])
                for i in range(1, count):
                    total = total + dot_tn(refs[at + i][:, where], refs[at + count + i][...])
                refs[-1][k * size : (k + 1) * size, start : start + n] = total.astype(bf16)
            at += 2 * count
            start += n

    flat = [v for lefts, rights in groups for v in (*lefts, *rights)]
    return pl.pallas_call(
        body,
        grid_spec=pltpu.PrefetchScalarGridSpec(
            num_scalar_prefetch=1,
            grid=(steps,),
            in_specs=[pl.BlockSpec(v.shape, lambda i, s: (0, 0)) for v in flat],
            out_specs=pl.BlockSpec((per_step * unit, sum(widths)), lambda i, s: (i, 0)),
        ),
        out_shape=like((width, sum(widths))),
        compiler_params=pltpu.CompilerParams(vmem_limit_bytes=VMEM_BYTES),
    )(jnp.asarray(np.concatenate(orders), jnp.int32), *flat)


def product_t(lefts, right, rows, add=None):
    count = len(lefts)
    tokens = lefts[0].shape[0]
    width, n = right.shape

    def body(*refs):
        right_ref = refs[count]
        total, start = None, 0
        for left in refs[:count]:
            stop = start + left.shape[1]
            part = dot_t(left[...], right_ref[:, start:stop])
            total = part if total is None else total + part
            start = stop
        if add is not None:
            total = total + refs[count + 1][...].astype(f32)
        refs[-1][...] = total.astype(bf16)

    block = pl.BlockSpec((tokens, rows), lambda i: (0, i))
    return pl.pallas_call(
        body,
        grid=(width // rows,),
        in_specs=[pl.BlockSpec(left.shape, lambda i: (0, 0)) for left in lefts]
        + [pl.BlockSpec((rows, n), lambda i: (i, 0))]
        + ([] if add is None else [block]),
        out_specs=block,
        out_shape=like((tokens, width)),
        compiler_params=pltpu.CompilerParams(vmem_limit_bytes=VMEM_BYTES),
    )(*lefts, right, *([] if add is None else [add]))


def feed_forward(normed, gate_up, dout, down):
    tokens, width = normed.shape
    units = down.shape[1]
    cols = 256
    steps = units // cols

    def body(normed_ref, gate_ref, up_ref, dout_ref, down_ref, inner_ref, d_gate_ref, d_up_ref):
        gate = dot(normed_ref[...], gate_ref[...])
        up = dot(normed_ref[...], up_ref[...])
        d_inner = dot(dout_ref[...], down_ref[...])
        s = jax.nn.sigmoid(gate)
        act = gate * s
        inner_ref[...] = (act * up).astype(bf16)
        d_gate_ref[...] = (d_inner * up * s * (1.0 + gate * (1.0 - s))).astype(bf16)
        d_up_ref[...] = (d_inner * act).astype(bf16)

    rows = pl.BlockSpec((tokens, width), lambda i: (0, 0))
    block = pl.BlockSpec((tokens, cols), lambda i: (0, i))
    return pl.pallas_call(
        body,
        grid=(steps,),
        in_specs=[
            rows,
            pl.BlockSpec((width, cols), lambda i: (0, i)),
            pl.BlockSpec((width, cols), lambda i: (0, steps + i)),
            rows,
            pl.BlockSpec((width, cols), lambda i: (0, i)),
        ],
        out_specs=[block] * 3,
        out_shape=[like((tokens, units))] * 3,
        compiler_params=pltpu.CompilerParams(vmem_limit_bytes=ALL_VMEM_BYTES),
    )(normed, gate_up, gate_up, dout, down)


def after(values, *others):
    return list(lax.optimization_barrier(tuple(values) + others))[: len(values)]


def on_device(
    tokens,
    block_pos,
    w_query,
    key_weight,
    value_weight,
    w_out,
    w_gate,
    w_up,
    w_down,
    attn_gain,
    mlp_gain,
    qk_gain,
    grad_out,
):
    g = Grid()
    A, R, Y = g.A, g.R, g.Y
    a, b, y, c = g.a, g.b, g.y, g.c
    pieces = R * Y
    rows_own = w_query.shape[0]
    width = tokens.shape[2]
    piece_width = width // pieces
    token_rows = tokens.shape[1]
    group_rows = A * token_rows
    score_scale = HEAD_SIZE ** (-0.5)
    q_cols = GROUP * HEAD_SIZE
    qkv_cols = q_cols + 2 * HEAD_SIZE
    ff_cols = FF // (2 * A)
    spot = jnp.stack([c, a]).astype(jnp.int32)

    unit = 2 * rows_own

    def permute(arrays, back):
        cuts = (R * Y, A, unit) if back else (A, R * Y, unit)
        columns = np.arange(width).reshape(cuts).transpose(1, 0, 2).reshape(-1)
        if unit % LANES == 0:
            return reorder(arrays, (columns[::LANES] // LANES).tolist())
        return [jnp.take(array, columns, axis=1) for array in arrays]

    places = jnp.stack(
        [(b - i) % R * Y + (y - j) % Y for i, j in g.pairs()]
    ).astype(jnp.int32)

    x_own, dout_own = tokens[0], grad_out[0]
    x_parts = g.gather_a(x_own, own_first=False)
    out_w = lax.all_gather(w_out, BOTH, axis=0, tiled=True)
    (cut,) = cut_columns([[w_query, key_weight, value_weight]], spot, A)
    packed = jnp.concatenate([attn_gain, mlp_gain, qk_gain.reshape(-1)])
    packed = jnp.stack(
        [jnp.pad(v, (0, qkv_cols - v.shape[0])) for v in (packed, block_pos[0].astype(bf16))]
    )
    packed = jnp.pad(packed, ((0, EXTRA - 2), (0, 0)))
    sent = jnp.concatenate([cut[1].reshape(A * rows_own, qkv_cols), packed])
    got = g.swap(sent)
    other_packed = got[A * rows_own :]
    qkv_local = merge_with_extra(
        cut[0],
        got[: A * rows_own].reshape(A, rows_own, qkv_cols),
        [packed, other_packed],
        spot,
    )
    qkv_piece = g.exchange_a(qkv_local).reshape(-1, qkv_cols)
    qkv_w, extras = stack_with_extra(g.spread(qkv_piece), places, A, unit, 2 * EXTRA)
    packed = extras.reshape(2 * A * pieces, EXTRA, qkv_cols)[:, 0].astype(f32)
    first_gain = packed[..., :rows_own].reshape(width)
    second_gain = packed[..., rows_own : 2 * rows_own].reshape(width)
    small = packed[..., 2 * rows_own : 2 * rows_own + 2 * (HEAD_SIZE // (2 * pieces * A))]
    small = jnp.transpose(small.reshape(2 * A * pieces, 2, -1), (1, 0, 2)).reshape(2, HEAD_SIZE)
    query_gain, key_gain = small[0], small[1]

    (cut,) = cut_columns([[w_gate, w_up, w_down]], after([spot], qkv_local)[0], A)
    gu_local, down_local = merge_rows(cut[0], g.swap(cut[1]), spot, [2 * ff_cols, ff_cols])
    (gu_local,) = after([gu_local], qkv_piece)
    gu_piece = g.exchange_a(gu_local).reshape(A * unit, 2 * ff_cols)
    (down_local,) = after([down_local], gu_piece)
    down_piece = g.exchange_a(down_local).reshape(A * unit, ff_cols)

    blocks_seen = block_pos.shape[1]
    orders = [block_pos[0], other_packed[1, :blocks_seen].astype(jnp.int32)]
    row_offsets = jnp.arange(token_rows, dtype=jnp.int32)

    def positions(order, shift):
        blocks = [order[part * R + (b - shift) % R] for part in range(A)]
        return jnp.concatenate([block * token_rows + row_offsets for block in blocks])

    local_pos = [positions(order, 0) for order in orders]
    key_pos = [jnp.concatenate([positions(order, i) for i in range(R)]) for order in orders]
    exponent = jnp.arange(HEAD_SIZE // 2, dtype=f32) * (-2.0 / HEAD_SIZE)
    angles = jnp.concatenate(local_pos).astype(f32)[:, None] * (rope_base**exponent)[None, :]
    cosine, sine = jnp.cos(angles), jnp.sin(angles)
    cosine3, sine3 = cosine[:, None, :], sine[:, None, :]

    x_group = stack_parts(x_parts, spot)
    inputs = x_group.astype(f32)
    x_root = inv_rms(inputs)
    normed_own = (inputs * x_root * first_gain).astype(bf16)
    normed = [normed_own, g.swap(normed_own)]
    made = jnp.concatenate([dot(part, qkv_w) for part in normed], axis=0)
    gu_by = g.gather_by(after([gu_piece], out_w, made)[0])
    down_w = g.gather_by(after([down_piece], gu_by)[0])
    q_pre = made[:, :q_cols].reshape(2 * group_rows, GROUP, HEAD_SIZE)
    k_pre = made[:, q_cols : q_cols + HEAD_SIZE]
    value = made[:, q_cols + HEAD_SIZE :].astype(bf16)
    q_root, k_root = inv_rms(q_pre), inv_rms(k_pre)
    query = rotate(q_pre * q_root * query_gain, cosine3, sine3).astype(bf16)
    key = rotate(k_pre * k_root * key_gain, cosine, sine).astype(bf16)
    key_values = jnp.concatenate([key, value], axis=1)
    key_values = [key_values] + [g.move(key_values, b=i) for i in range(1, R)]

    def of_sequence(array, n):
        return array[n * group_rows : (n + 1) * group_rows]

    keys = [
        jnp.concatenate([of_sequence(kv, n)[:, :HEAD_SIZE] for kv in key_values]) for n in range(2)
    ]
    values = [
        jnp.concatenate([of_sequence(kv, n)[:, HEAD_SIZE:] for kv in key_values]) for n in range(2)
    ]

    visible = [local_pos[n][:, None] >= key_pos[n][None, :] for n in range(2)]

    def attend(n):
        scores = jnp.einsum(
            "qgd,td->gqt", of_sequence(query, n), keys[n], preferred_element_type=f32
        )
        scores = jnp.where(visible[n], scores * score_scale, -1e30)
        top = jnp.max(scores, axis=-1, keepdims=True)
        weights = jnp.exp(scores - top)
        totals = jnp.sum(weights, axis=-1, keepdims=True)
        log_total = top + jnp.log(totals)
        mixed = jnp.einsum(
            "gqt,td->gqd", weights.astype(bf16), values[n], preferred_element_type=f32
        )
        return mixed / totals, log_total

    def flat(heads):
        return jnp.transpose(heads, (1, 0, 2)).reshape(group_rows, q_cols).astype(bf16)

    mixed_other = attend(1)
    got = g.swap(flat(mixed_other[0]))
    mixed = [attend(0), mixed_other]
    attended = jnp.concatenate([flat(mixed[0][0]), got], axis=1)
    (attended,) = after([attended], down_piece)
    att_parts = g.gather_a(attended)
    att_heads = gather_heads(after(att_parts, gu_by), spot, q_cols)

    (dout_by,) = permute(after([dout_own], att_parts[-1]), False)
    middle = inputs + dot_t(att_heads, out_w)
    dout_parts = g.gather_a(dout_by, False, (middle,))
    root2 = inv_rms(middle)
    normed2_own = (middle * root2 * second_gain).astype(bf16)
    (normed2_own,) = permute([normed2_own], False)
    normed2 = [normed2_own, g.swap(normed2_own)]
    dout_group = stack_parts(dout_parts, spot)
    dout = [dout_group, g.swap(dout_group)]
    fed = [feed_forward(normed2[n], gu_by, dout[n], down_w) for n in range(2)]
    inner = [f[0] for f in fed]
    d_gu = [f[1:] for f in fed]

    def of_both(parts, weight):
        got = g.swap(product_t(parts[1], weight, 512))
        return product_t(parts[0], weight, 512, got)

    def own_rows(array):
        return lax.dynamic_slice_in_dim(array, a * token_rows, token_rows, axis=0)

    d_normed2 = of_both(d_gu, gu_by)
    (e2,) = permute([g.to_rows_owner(d_normed2)], True)
    middle_own, root2_own = own_rows(middle), own_rows(root2)
    mlp_gain_grad = jnp.sum(e2 * middle_own * root2_own, axis=0)
    grad_middle = dout_own.astype(f32) + norm_back(middle_own, root2_own, second_gain, e2)

    by_order = np.arange(R * A * Y).reshape(A, R * Y).T.reshape(-1)

    def over_tokens(*groups):
        if unit % LANES == 0:
            orders = [by_order if natural else np.arange(R * A * Y) for _, _, natural in groups]
            return token_products([group[:2] for group in groups], orders)
        made = []
        for lefts, rights, natural in groups:
            total = dot_tn(lefts[0], rights[0]) + dot_tn(lefts[1], rights[1])
            total = total.reshape(R * A * Y, unit, -1)
            made.append(jnp.take(total, by_order, axis=0) if natural else total)
        return jnp.concatenate(made, axis=-1).reshape(width, -1).astype(bf16)

    def to_owner(dealt, widths):
        keep = lax.dynamic_index_in_dim(dealt, c, 1, keepdims=False)
        send = lax.dynamic_index_in_dim(dealt, 1 - c, 1, keepdims=False)
        return join_columns(keep, g.swap(send), spot, widths)

    def part_rows(total):
        return total.reshape(A, unit, -1)

    def core_rows(dealt):
        return dealt.reshape(A, 2, rows_own, -1)

    later = after(normed2, d_normed2)
    mlp_grad = over_tokens(
        (later, [d[0] for d in d_gu], False),
        (later, [d[1] for d in d_gu], False),
        (dout, inner, False),
    )
    mlp_total = g.scatter("by", mlp_grad)
    out_part = of_both([[v] for v in after(inner, d_normed2)], down_w)

    d_branch = grad_middle.astype(bf16)
    d_att = dot(d_branch, out_w).astype(bf16)
    if pieces * unit % LANES == 0:
        dealt = column_blocks([d_att, d_branch], A)
    else:
        dealt = jnp.concatenate([d_att.reshape(token_rows, A, -1), d_branch.reshape(token_rows, A, -1)], -1)
        dealt = jnp.swapaxes(dealt, 0, 1)
    dealt = g.exchange_a(dealt).reshape(group_rows, -1)
    d_att, rows_of_part = dealt[:, : 2 * q_cols], dealt[:, 2 * q_cols :]
    out_mine = g.scatter("a", after([out_part], mlp_total, d_att)[0])
    mlp_dealt = g.exchange_a(after([part_rows(mlp_total)], d_att)[0])
    mine_half, other_half = g.by_core(d_att[:, :q_cols], d_att[:, q_cols:])
    d_att = [mine_half, g.swap(other_half)]

    def attend_back(n):
        d_mixed = d_att[n].reshape(group_rows, GROUP, HEAD_SIZE)
        o, log_total = mixed[n]
        delta = jnp.sum(jnp.transpose(d_mixed, (1, 0, 2)).astype(f32) * o, axis=-1, keepdims=True)
        q = of_sequence(query, n)
        scores = jnp.einsum("qgd,td->gqt", q, keys[n], preferred_element_type=f32)
        scores = jnp.where(visible[n], scores * score_scale, -1e30)
        weights = jnp.exp(scores - log_total)
        d_weights = jnp.einsum("qgd,td->gqt", d_mixed, values[n], preferred_element_type=f32)
        d_scores = (weights * (d_weights - delta)).astype(bf16)
        d_query = jnp.einsum("gqt,td->qgd", d_scores, keys[n], preferred_element_type=f32)
        d_key = jnp.einsum("gqt,qgd->td", d_scores, q, preferred_element_type=f32)
        d_value = jnp.einsum(
            "gqt,qgd->td", weights.astype(bf16), d_mixed, preferred_element_type=f32
        )
        return d_query * score_scale, jnp.concatenate([d_key * score_scale, d_value], axis=1)

    backs = [attend_back(0), attend_back(1)]
    d_query = jnp.concatenate([back[0] for back in backs], axis=0)
    d_kv = jnp.concatenate([of_sequence(back[1], 0) for back in backs], axis=0)
    for i in range(1, R):
        block = jnp.concatenate([of_sequence(back[1], i) for back in backs], axis=0)
        d_kv = d_kv + g.move(block.astype(bf16), b=-i).astype(f32)
    (d_kv,) = after([d_kv], mlp_dealt)
    e_q = unrotate(d_query, cosine3, sine3)
    e_k = unrotate(d_kv[:, :HEAD_SIZE], cosine, sine)
    d_q_pre = norm_back(q_pre, q_root, query_gain, e_q).reshape(2 * group_rows, q_cols)
    d_k_pre = norm_back(k_pre, k_root, key_gain, e_k)
    qk_gain_grad = jnp.stack(
        [jnp.sum(e_q * q_pre * q_root, axis=(0, 1)), jnp.sum(e_k * k_pre * k_root, axis=0)]
    )
    d_qkv = jnp.concatenate([d_q_pre, d_k_pre, d_kv[:, HEAD_SIZE:]], axis=1).astype(bf16)
    d_qkv = [of_sequence(d_qkv, 0), of_sequence(d_qkv, 1)]
    qkv_grad = over_tokens((normed, d_qkv, True))
    d_qkv = after(d_qkv, qkv_grad)
    d_normed = of_both([[v] for v in d_qkv], qkv_w)
    (out_sum,) = permute([after([out_mine], d_normed)[0].astype(f32)], True)
    result = (middle_own + out_sum).astype(bf16)
    qkv_total = g.scatter("by", qkv_grad)
    attn_gain_grad = jnp.sum(d_normed * inputs * x_root, axis=0)
    e1 = g.to_rows_owner(d_normed)
    grad_input = grad_middle + norm_back(
        x_own.astype(f32), inv_rms(x_own.astype(f32)), first_gain, e1
    )

    (qkv_total,) = after([qkv_total], e1)
    dealt = core_rows(g.exchange_a(part_rows(qkv_total)))
    grad_wq, grad_wk, grad_wv = to_owner(dealt, [q_cols, HEAD_SIZE, HEAD_SIZE])

    def by_first(array):
        return jnp.swapaxes(array, 0, 1).reshape(pieces, A, 2, -1)

    small = qk_gain_grad.reshape(2, A, pieces, 2, -1)
    small = jnp.transpose(small, (2, 1, 3, 0, 4)).reshape(pieces, A, 2, -1)
    sums = jnp.concatenate(
        [
            by_first(attn_gain_grad.reshape(A, pieces, 2, rows_own)),
            by_first(mlp_gain_grad.reshape(A, pieces, 2, rows_own)),
            small,
        ],
        axis=-1,
    )
    keep = lax.dynamic_index_in_dim(sums, c, 2, keepdims=False)
    send = lax.dynamic_index_in_dim(sums, 1 - c, 2, keepdims=False)
    sums = g.collect(keep + g.swap(send))
    sums = sum(g.deal_a(g.ahead(sums)))
    sums = [
        sums[:rows_own],
        sums[rows_own : 2 * rows_own],
        sums[2 * rows_own :].reshape(2, -1),
    ]

    (rows_of_part,) = after([rows_of_part], d_kv)
    grad_wo = g.scatter("byc", dot_tn(rows_of_part, att_heads).astype(bf16)).astype(f32)
    grad_wg, grad_wu, grad_wd = to_owner(core_rows(mlp_dealt), [ff_cols] * 3)
    return (
        result[None],
        grad_input[None],
        grad_wq,
        grad_wk,
        grad_wv,
        grad_wo,
        grad_wg,
        grad_wu,
        grad_wd,
        *sums,
    )


def solution(mesh):
    placed = (
        P("fsdp", "seq", None),
        P("fsdp", None),
        P(("seq", "fsdp"), None),
        P(("seq", "fsdp"), None),
        P(("seq", "fsdp"), None),
        P(("seq", "fsdp"), None),
        P(("seq", "fsdp"), None),
        P(("seq", "fsdp"), None),
        P(("seq", "fsdp"), None),
        P(("seq", "fsdp")),
        P(("seq", "fsdp")),
        P(None, ("seq", "fsdp")),
        P("fsdp", "seq", None),
    )
    return jax.shard_map(
        on_device,
        mesh=mesh,
        in_specs=placed,
        out_specs=(
            P("fsdp", "seq", None),
            P("fsdp", "seq", None),
            P(("seq", "fsdp"), None),
            P(("seq", "fsdp"), None),
            P(("seq", "fsdp"), None),
            P(("seq", "fsdp"), None),
            P(("seq", "fsdp"), None),
            P(("seq", "fsdp"), None),
            P(("seq", "fsdp"), None),
            P(("seq", "fsdp")),
            P(("seq", "fsdp")),
            P(None, ("seq", "fsdp")),
        ),
        check_vma=False,
    )
```

```python
import jax
import jax.numpy as jnp
import numpy as np
from jax import lax
from jax.experimental import pallas as pl
from jax.experimental.pallas import tpu as pltpu
from jax.sharding import PartitionSpec as P

QUERY_HEADS = 16
KEY_VALUE_HEADS = 8
HEAD_SIZE = 128
FF = 6144

rope_base = 1000000.0
norm_eps = 1e-06
BOTH = ("seq", "fsdp")
bf16 = jnp.bfloat16
f32 = jnp.float32

PARTS = KEY_VALUE_HEADS // 2
GROUP = QUERY_HEADS // KEY_VALUE_HEADS


LANES = 128
EXTRA = 16
VMEM_BYTES = 48 * 1024 * 1024
ALL_VMEM_BYTES = 60 * 1024 * 1024


def dot(left, right):
    return jnp.dot(left, right, preferred_element_type=f32)


def dot_t(left, right):
    return lax.dot_general(left, right, (((1,), (1,)), ((), ())), preferred_element_type=f32)


def dot_tn(left, right):
    return lax.dot_general(left, right, (((0,), (0,)), ((), ())), preferred_element_type=f32)


def inv_rms(tensor):
    return lax.rsqrt(jnp.mean(tensor * tensor, axis=-1, keepdims=True) + norm_eps)


def norm_back(tensor, root, gain, incoming):
    scaled = gain * incoming
    return root * scaled - tensor * (root * root * root) * jnp.mean(
        scaled * tensor, axis=-1, keepdims=True
    )


def halves(tensor):
    half_width = tensor.shape[-1] // 2
    return tensor[..., :half_width], tensor[..., half_width:]


def rotate(tensor, cosine, sine):
    front, back = halves(tensor)
    return jnp.concatenate([front * cosine - back * sine, back * cosine + front * sine], axis=-1)


def unrotate(tensor, cosine, sine):
    front, back = halves(tensor)
    return jnp.concatenate([front * cosine + back * sine, back * cosine - front * sine], axis=-1)


class Grid:
    def __init__(self):
        self.fsdp = lax.axis_size("fsdp")
        self.A = PARTS
        self.R = lax.axis_size("seq") // self.A
        self.Y = self.fsdp // 2
        s, f = lax.axis_index("seq"), lax.axis_index("fsdp")
        self.a, self.b = s // self.R, s % self.R
        self.y, self.c = f // 2, f % 2
        self.places = [
            (a, b, y, c)
            for a in range(self.A)
            for b in range(self.R)
            for y in range(self.Y)
            for c in range(2)
        ]

    def at(self, a, b, y, c):
        return (a * self.R + b % self.R) * self.fsdp + (y % self.Y) * 2 + c % 2

    def groups(self, along):
        found = {}
        for place in self.places:
            fixed = tuple(v for v, name in zip(place, "abyc") if name not in along)
            found.setdefault(fixed, []).append(self.at(*place))
        return list(found.values())

    def move(self, array, a=0, b=0, y=0, c=0):
        route = [
            (self.at(*p), self.at(p[0] ^ a, p[1] + b, p[2] + y, p[3] + c)) for p in self.places
        ]
        return lax.ppermute(array, BOTH, route)

    def swap(self, array):
        return self.move(array, c=1)

    def exchange_a(self, array):
        return lax.all_to_all(array, BOTH, 0, 0, axis_index_groups=self.groups("a"), tiled=True)

    def gather_by(self, array):
        return lax.all_gather(array, BOTH, axis_index_groups=self.groups("by"), axis=0, tiled=True)

    def scatter(self, along, array):
        return lax.psum_scatter(
            array, BOTH, axis_index_groups=self.groups(along), scatter_dimension=0, tiled=True
        )

    def deal_a(self, blocks):
        return [blocks[0]] + [self.move(blocks[d], a=d) for d in range(1, self.A)]

    def gather_a(self, array, own_first=True, then=()):
        held = {0: array}
        bit = self.A // 2
        while bit:
            own = self.move(array, a=bit)
            rest = [d for d in held if d]
            sent = [held[d] for d in rest]
            sent = after(sent, *((own,) if own_first else then)) if rest else sent
            held[bit] = own
            held.update({d | bit: self.move(v, a=bit) for d, v in zip(rest, sent)})
            bit //= 2
        return [held[d] for d in range(self.A)]

    def ahead(self, array):
        return [
            lax.dynamic_index_in_dim(array, self.a ^ d, 0, keepdims=False) for d in range(self.A)
        ]

    def in_place(self, blocks):
        held = jnp.stack(blocks)
        return jnp.stack(
            [
                lax.dynamic_index_in_dim(held, self.a ^ part, 0, keepdims=False)
                for part in range(self.A)
            ]
        )

    def by_core(self, first, second):
        return (
            jnp.where(self.c == 0, first, second),
            jnp.where(self.c == 0, second, first),
        )

    def pairs(self):
        return [(i, j) for i in range(self.R) for j in range(self.Y)]

    def spread(self, piece):
        return [piece] + [self.move(piece, b=i, y=j) for i, j in self.pairs()[1:]]

    def mine_first(self, pieces):
        return [
            lax.dynamic_index_in_dim(
                pieces, (self.b - i) % self.R * self.Y + (self.y - j) % self.Y, 0, False
            )
            for i, j in self.pairs()
        ]

    def collect(self, pieces, *late):
        held = self.mine_first(pieces)
        got = [self.move(part, b=-i, y=-j) for part, (i, j) in zip(held[1:], self.pairs()[1:])]
        got = after(got, *late) if late else got
        return added(held[0], got)

    def to_rows_owner(self, partial):
        got = self.exchange_a(partial.reshape(self.A, -1, partial.shape[1]))
        return added(got[0], list(got[1:]))


def added(first, rest):
    total = first.astype(f32)
    for part in rest:
        total = total + part.astype(f32)
    return total


def whole_call(body, scalars, ins, outs):
    return pl.pallas_call(
        body,
        grid_spec=pltpu.PrefetchScalarGridSpec(
            num_scalar_prefetch=1,
            grid=(1,),
            in_specs=[pl.BlockSpec(v.shape, lambda i, s, n=v.ndim: (0,) * n) for v in ins],
            out_specs=[pl.BlockSpec(v.shape, lambda i, s, n=len(v.shape): (0,) * n) for v in outs],
        ),
        out_shape=outs,
        compiler_params=pltpu.CompilerParams(vmem_limit_bytes=VMEM_BYTES),
    )(scalars, *ins)


def like(shape, kind=bf16):
    return jax.ShapeDtypeStruct(shape, kind)


def at_multiple(number, size):
    return pl.ds(pl.multiple_of(number * size, size), size)


def reorder(arrays, source):
    count = len(arrays)

    def body(_, *refs):
        for i, at in enumerate(source):
            for src, dst in zip(refs[:count], refs[count:]):
                dst[:, i * LANES : (i + 1) * LANES] = src[:, at * LANES : (at + 1) * LANES]

    return whole_call(
        body, jnp.zeros((1,), jnp.int32), arrays, [like(v.shape, v.dtype) for v in arrays]
    )


def cut_columns(groups, spot, parts):
    flat = [a for group in groups for a in group]
    rows = flat[0].shape[0]
    widths = [a.shape[1] // (2 * parts) for a in flat]
    group_widths = [sum(a.shape[1] // (2 * parts) for a in group) for group in groups]

    def body(spot_ref, *refs):
        ins, outs = refs[: len(flat)], refs[len(flat) :]
        for half in range(2):
            core = spot_ref[0] if half == 0 else 1 - spot_ref[0]
            at = 0
            for k, group in enumerate(groups):
                start = 0
                for _ in group:
                    n = widths[at]
                    outs[2 * k + half][0, :, start : start + n] = ins[at][:, at_multiple(core, n)]
                    start += n
                    at += 1

    out_specs, out_shape = [], []
    for n in group_widths:
        for _ in range(2):
            out_specs.append(pl.BlockSpec((1, rows, n), lambda i, spot: (i, 0, 0)))
            out_shape.append(like((parts, rows, n)))
    made = pl.pallas_call(
        body,
        grid_spec=pltpu.PrefetchScalarGridSpec(
            num_scalar_prefetch=1,
            grid=(parts,),
            in_specs=[pl.BlockSpec((rows, 2 * n), lambda i, spot: (0, i)) for n in widths],
            out_specs=out_specs,
        ),
        out_shape=out_shape,
        compiler_params=pltpu.CompilerParams(vmem_limit_bytes=ALL_VMEM_BYTES),
    )(spot, *flat)
    return [(made[2 * k], made[2 * k + 1]) for k in range(len(groups))]


def merge_with_extra(keep, got, extras, spot):
    parts, rows, n = keep.shape
    more = extras[0].shape[0]

    def body(spot_ref, keep_ref, got_ref, own_ref, other_ref, out):
        here, there = spot_ref[0], 1 - spot_ref[0]
        for part in range(parts):
            out[part, at_multiple(here, rows), :] = keep_ref[part]
            out[part, at_multiple(there, rows), :] = got_ref[part]
            for core, ref in ((here, own_ref), (there, other_ref)):
                where = pl.ds(pl.multiple_of(2 * rows + core * more, more), more)
                out[part, where, :] = ref[...]

    return whole_call(
        body, spot, [keep, got, *extras], [like((parts, 2 * (rows + more), n))]
    )[0]


def merge_rows(keep, got, spot, widths):
    parts, rows, _ = keep.shape

    def body(spot_ref, keep_ref, got_ref, *outs):
        for part in range(parts):
            for core, ref in ((spot_ref[0], keep_ref), (1 - spot_ref[0], got_ref)):
                start = 0
                for n, out in zip(widths, outs):
                    out[part, at_multiple(core, rows), :] = ref[part, :, start : start + n]
                    start += n

    return whole_call(body, spot, [keep, got], [like((parts, 2 * rows, n)) for n in widths])


def stack_parts(blocks, spot):
    parts = len(blocks)
    rows, n = blocks[0].shape

    def body(spot_ref, *refs):
        for d in range(parts):
            refs[parts][at_multiple(spot_ref[1] ^ d, rows), :] = refs[d][...]

    return whole_call(body, spot, blocks, [like((parts * rows, n))])[0]


def stack_with_extra(blocks, where, parts, rows, more):
    n = blocks[0].shape[1]

    def body(where_ref, *refs):
        for k in range(len(blocks)):
            for part in range(parts):
                start = part * (rows + more)
                place = part * len(blocks) + where_ref[k]
                refs[-2][at_multiple(place, rows), :] = refs[k][start : start + rows, :]
                refs[-1][at_multiple(place, more), :] = refs[k][start + rows : start + rows + more, :]

    total = len(blocks) * parts
    return whole_call(body, where, blocks, [like((total * rows, n)), like((total * more, n))])


def gather_heads(blocks, spot, half):
    parts = len(blocks)
    tokens = blocks[0].shape[0]

    def body(spot_ref, *refs):
        for d in range(parts):
            for k, core in enumerate((spot_ref[0], 1 - spot_ref[0])):
                where = at_multiple(2 * (spot_ref[1] ^ d) + core, half)
                refs[-1][:, where] = refs[d][:, k * half : (k + 1) * half]

    return whole_call(body, spot, blocks, [like((tokens, 2 * parts * half))])[0]


def column_blocks(arrays, parts):
    rows = arrays[0].shape[0]
    widths = [array.shape[1] // parts for array in arrays]

    def body(_, *refs):
        for part in range(parts):
            start = 0
            for n, src in zip(widths, refs):
                refs[-1][part, :, start : start + n] = src[:, part * n : (part + 1) * n]
                start += n

    return whole_call(
        body, jnp.zeros((1,), jnp.int32), arrays, [like((parts, rows, sum(widths)))]
    )[0]


def join_columns(keep, got, spot, widths):
    parts, rows, total = keep.shape

    def body(spot_ref, keep_ref, got_ref, *outs):
        mine = pl.program_id(1) == spot_ref[0]
        start = 0
        for n, out in zip(widths, outs):
            part = slice(start, start + n)
            out[...] = jnp.where(mine, keep_ref[0, :, part], got_ref[0, :, part]).astype(f32)
            start += n

    block = pl.BlockSpec((1, rows, total), lambda i, h, spot: (i, 0, 0))
    return pl.pallas_call(
        body,
        grid_spec=pltpu.PrefetchScalarGridSpec(
            num_scalar_prefetch=1,
            grid=(parts, 2),
            in_specs=[block, block],
            out_specs=[pl.BlockSpec((rows, n), lambda i, h, spot: (0, 2 * i + h)) for n in widths],
        ),
        out_shape=[like((rows, 2 * parts * n), f32) for n in widths],
        compiler_params=pltpu.CompilerParams(vmem_limit_bytes=VMEM_BYTES),
    )(spot, keep, got)


def token_products(groups, orders):
    counts = [len(lefts) for lefts, _ in groups]
    tokens, width = groups[0][0][0].shape
    widths = [rights[0].shape[1] for _, rights in groups]
    blocks = len(orders[0])
    unit = width // blocks
    steps = min(4, blocks)
    per_step = blocks // steps

    in_turn = [bool(np.array_equal(order, np.arange(blocks))) for order in orders]

    def body(order_ref, *refs):
        at, start = 0, 0
        for m, (count, n) in enumerate(zip(counts, widths)):
            first = pl.program_id(0) * per_step
            if in_turn[m]:
                places = [at_multiple(pl.program_id(0), per_step * unit)]
            else:
                places = [
                    at_multiple(order_ref[m * blocks + first + k], unit) for k in range(per_step)
                ]
            size = per_step * unit // len(places)
            for k, where in enumerate(places):
                total = dot_tn(refs[at][:, where], refs[at + count][...])
                for i in range(1, count):
                    total = total + dot_tn(refs[at + i][:, where], refs[at + count + i][...])
                refs[-1][k * size : (k + 1) * size, start : start + n] = total.astype(bf16)
            at += 2 * count
            start += n

    flat = [v for lefts, rights in groups for v in (*lefts, *rights)]
    return pl.pallas_call(
        body,
        grid_spec=pltpu.PrefetchScalarGridSpec(
            num_scalar_prefetch=1,
            grid=(steps,),
            in_specs=[pl.BlockSpec(v.shape, lambda i, s: (0, 0)) for v in flat],
            out_specs=pl.BlockSpec((per_step * unit, sum(widths)), lambda i, s: (i, 0)),
        ),
        out_shape=like((width, sum(widths))),
        compiler_params=pltpu.CompilerParams(vmem_limit_bytes=VMEM_BYTES),
    )(jnp.asarray(np.concatenate(orders), jnp.int32), *flat)


def product_t(lefts, right, rows, add=None):
    count = len(lefts)
    tokens = lefts[0].shape[0]
    width, n = right.shape

    def body(*refs):
        right_ref = refs[count]
        total, start = None, 0
        for left in refs[:count]:
            stop = start + left.shape[1]
            part = dot_t(left[...], right_ref[:, start:stop])
            total = part if total is None else total + part
            start = stop
        if add is not None:
            total = total + refs[count + 1][...].astype(f32)
        refs[-1][...] = total.astype(bf16)

    block = pl.BlockSpec((tokens, rows), lambda i: (0, i))
    return pl.pallas_call(
        body,
        grid=(width // rows,),
        in_specs=[pl.BlockSpec(left.shape, lambda i: (0, 0)) for left in lefts]
        + [pl.BlockSpec((rows, n), lambda i: (i, 0))]
        + ([] if add is None else [block]),
        out_specs=block,
        out_shape=like((tokens, width)),
        compiler_params=pltpu.CompilerParams(vmem_limit_bytes=VMEM_BYTES),
    )(*lefts, right, *([] if add is None else [add]))


def feed_forward(normed, gate_up, dout, down):
    tokens, width = normed.shape
    units = down.shape[1]
    cols = 256
    steps = units // cols

    def body(normed_ref, gate_ref, up_ref, dout_ref, down_ref, inner_ref, d_gate_ref, d_up_ref):
        gate = dot(normed_ref[...], gate_ref[...])
        up = dot(normed_ref[...], up_ref[...])
        d_inner = dot(dout_ref[...], down_ref[...])
        s = jax.nn.sigmoid(gate)
        act = gate * s
        inner_ref[...] = (act * up).astype(bf16)
        d_gate_ref[...] = (d_inner * up * s * (1.0 + gate * (1.0 - s))).astype(bf16)
        d_up_ref[...] = (d_inner * act).astype(bf16)

    rows = pl.BlockSpec((tokens, width), lambda i: (0, 0))
    block = pl.BlockSpec((tokens, cols), lambda i: (0, i))
    return pl.pallas_call(
        body,
        grid=(steps,),
        in_specs=[
            rows,
            pl.BlockSpec((width, cols), lambda i: (0, i)),
            pl.BlockSpec((width, cols), lambda i: (0, steps + i)),
            rows,
            pl.BlockSpec((width, cols), lambda i: (0, i)),
        ],
        out_specs=[block] * 3,
        out_shape=[like((tokens, units))] * 3,
        compiler_params=pltpu.CompilerParams(vmem_limit_bytes=ALL_VMEM_BYTES),
    )(normed, gate_up, gate_up, dout, down)


def after(values, *others):
    return list(lax.optimization_barrier(tuple(values) + others))[: len(values)]


def on_device(
    tokens,
    block_pos,
    w_query,
    key_weight,
    value_weight,
    w_out,
    w_gate,
    w_up,
    w_down,
    attn_gain,
    mlp_gain,
    qk_gain,
    grad_out,
):
    g = Grid()
    A, R, Y = g.A, g.R, g.Y
    a, b, y, c = g.a, g.b, g.y, g.c
    pieces = R * Y
    rows_own = w_query.shape[0]
    width = tokens.shape[2]
    piece_width = width // pieces
    token_rows = tokens.shape[1]
    group_rows = A * token_rows
    score_scale = HEAD_SIZE ** (-0.5)
    q_cols = GROUP * HEAD_SIZE
    qkv_cols = q_cols + 2 * HEAD_SIZE
    ff_cols = FF // (2 * A)
    spot = jnp.stack([c, a]).astype(jnp.int32)

    unit = 2 * rows_own

    def permute(arrays, back):
        cuts = (R * Y, A, unit) if back else (A, R * Y, unit)
        columns = np.arange(width).reshape(cuts).transpose(1, 0, 2).reshape(-1)
        if unit % LANES == 0:
            return reorder(arrays, (columns[::LANES] // LANES).tolist())
        return [jnp.take(array, columns, axis=1) for array in arrays]

    places = jnp.stack(
        [(b - i) % R * Y + (y - j) % Y for i, j in g.pairs()]
    ).astype(jnp.int32)

    x_own, dout_own = tokens[0], grad_out[0]
    x_parts = g.gather_a(x_own, own_first=False)
    out_w = lax.all_gather(w_out, BOTH, axis=0, tiled=True)
    (cut,) = cut_columns([[w_query, key_weight, value_weight]], spot, A)
    packed = jnp.concatenate([attn_gain, mlp_gain, qk_gain.reshape(-1)])
    packed = jnp.stack(
        [jnp.pad(v, (0, qkv_cols - v.shape[0])) for v in (packed, block_pos[0].astype(bf16))]
    )
    packed = jnp.pad(packed, ((0, EXTRA - 2), (0, 0)))
    sent = jnp.concatenate([cut[1].reshape(A * rows_own, qkv_cols), packed])
    got = g.swap(sent)
    other_packed = got[A * rows_own :]
    qkv_local = merge_with_extra(
        cut[0],
        got[: A * rows_own].reshape(A, rows_own, qkv_cols),
        [packed, other_packed],
        spot,
    )
    qkv_piece = g.exchange_a(qkv_local).reshape(-1, qkv_cols)
    qkv_w, extras = stack_with_extra(g.spread(qkv_piece), places, A, unit, 2 * EXTRA)
    packed = extras.reshape(2 * A * pieces, EXTRA, qkv_cols)[:, 0].astype(f32)
    first_gain = packed[..., :rows_own].reshape(width)
    second_gain = packed[..., rows_own : 2 * rows_own].reshape(width)
    small = packed[..., 2 * rows_own : 2 * rows_own + 2 * (HEAD_SIZE // (2 * pieces * A))]
    small = jnp.transpose(small.reshape(2 * A * pieces, 2, -1), (1, 0, 2)).reshape(2, HEAD_SIZE)
    query_gain, key_gain = small[0], small[1]

    (cut,) = cut_columns([[w_gate, w_up, w_down]], after([spot], qkv_local)[0], A)
    gu_local, down_local = merge_rows(cut[0], g.swap(cut[1]), spot, [2 * ff_cols, ff_cols])
    (gu_local,) = after([gu_local], qkv_piece)
    gu_piece = g.exchange_a(gu_local).reshape(A * unit, 2 * ff_cols)
    (down_local,) = after([down_local], gu_piece)
    down_piece = g.exchange_a(down_local).reshape(A * unit, ff_cols)

    blocks_seen = block_pos.shape[1]
    orders = [block_pos[0], other_packed[1, :blocks_seen].astype(jnp.int32)]
    row_offsets = jnp.arange(token_rows, dtype=jnp.int32)

    def positions(order, shift):
        blocks = [order[part * R + (b - shift) % R] for part in range(A)]
        return jnp.concatenate([block * token_rows + row_offsets for block in blocks])

    local_pos = [positions(order, 0) for order in orders]
    key_pos = [jnp.concatenate([positions(order, i) for i in range(R)]) for order in orders]
    exponent = jnp.arange(HEAD_SIZE // 2, dtype=f32) * (-2.0 / HEAD_SIZE)
    angles = jnp.concatenate(local_pos).astype(f32)[:, None] * (rope_base**exponent)[None, :]
    cosine, sine = jnp.cos(angles), jnp.sin(angles)
    cosine3, sine3 = cosine[:, None, :], sine[:, None, :]

    x_group = stack_parts(x_parts, spot)
    inputs = x_group.astype(f32)
    x_root = inv_rms(inputs)
    normed_own = (inputs * x_root * first_gain).astype(bf16)
    normed = [normed_own, g.swap(normed_own)]
    made = jnp.concatenate([dot(part, qkv_w) for part in normed], axis=0)
    gu_by = g.gather_by(after([gu_piece], out_w, made)[0])
    down_w = g.gather_by(after([down_piece], gu_by)[0])
    q_pre = made[:, :q_cols].reshape(2 * group_rows, GROUP, HEAD_SIZE)
    k_pre = made[:, q_cols : q_cols + HEAD_SIZE]
    value = made[:, q_cols + HEAD_SIZE :].astype(bf16)
    q_root, k_root = inv_rms(q_pre), inv_rms(k_pre)
    query = rotate(q_pre * q_root * query_gain, cosine3, sine3).astype(bf16)
    key = rotate(k_pre * k_root * key_gain, cosine, sine).astype(bf16)
    key_values = jnp.concatenate([key, value], axis=1)
    key_values = [key_values] + [g.move(key_values, b=i) for i in range(1, R)]

    def of_sequence(array, n):
        return array[n * group_rows : (n + 1) * group_rows]

    keys = [
        jnp.concatenate([of_sequence(kv, n)[:, :HEAD_SIZE] for kv in key_values]) for n in range(2)
    ]
    values = [
        jnp.concatenate([of_sequence(kv, n)[:, HEAD_SIZE:] for kv in key_values]) for n in range(2)
    ]

    visible = [local_pos[n][:, None] >= key_pos[n][None, :] for n in range(2)]

    def attend(n):
        scores = jnp.einsum(
            "qgd,td->gqt", of_sequence(query, n), keys[n], preferred_element_type=f32
        )
        scores = jnp.where(visible[n], scores * score_scale, -1e30)
        top = jnp.max(scores, axis=-1, keepdims=True)
        weights = jnp.exp(scores - top)
        totals = jnp.sum(weights, axis=-1, keepdims=True)
        log_total = top + jnp.log(totals)
        mixed = jnp.einsum(
            "gqt,td->gqd", weights.astype(bf16), values[n], preferred_element_type=f32
        )
        return mixed / totals, log_total

    def flat(heads):
        return jnp.transpose(heads, (1, 0, 2)).reshape(group_rows, q_cols).astype(bf16)

    mixed_other = attend(1)
    got = g.swap(flat(mixed_other[0]))
    mixed = [attend(0), mixed_other]
    attended = jnp.concatenate([flat(mixed[0][0]), got], axis=1)
    (attended,) = after([attended], down_piece)
    att_parts = g.gather_a(attended)
    att_heads = gather_heads(after(att_parts, gu_by), spot, q_cols)

    (dout_by,) = permute(after([dout_own], att_parts[-1]), False)
    middle = inputs + dot_t(att_heads, out_w)
    dout_parts = g.gather_a(dout_by, False, (middle,))
    root2 = inv_rms(middle)
    normed2_own = (middle * root2 * second_gain).astype(bf16)
    (normed2_own,) = permute([normed2_own], False)
    normed2 = [normed2_own, g.swap(normed2_own)]
    dout_group = stack_parts(dout_parts, spot)
    dout = [dout_group, g.swap(dout_group)]
    fed = [feed_forward(normed2[n], gu_by, dout[n], down_w) for n in range(2)]
    inner = [f[0] for f in fed]
    d_gu = [f[1:] for f in fed]

    def of_both(parts, weight):
        got = g.swap(product_t(parts[1], weight, 512))
        return product_t(parts[0], weight, 512, got)

    def own_rows(array):
        return lax.dynamic_slice_in_dim(array, a * token_rows, token_rows, axis=0)

    d_normed2 = of_both(d_gu, gu_by)
    (e2,) = permute([g.to_rows_owner(d_normed2)], True)
    middle_own, root2_own = own_rows(middle), own_rows(root2)
    mlp_gain_grad = jnp.sum(e2 * middle_own * root2_own, axis=0)
    grad_middle = dout_own.astype(f32) + norm_back(middle_own, root2_own, second_gain, e2)

    by_order = np.arange(R * A * Y).reshape(A, R * Y).T.reshape(-1)

    def over_tokens(*groups):
        if unit % LANES == 0:
            orders = [by_order if natural else np.arange(R * A * Y) for _, _, natural in groups]
            return token_products([group[:2] for group in groups], orders)
        made = []
        for lefts, rights, natural in groups:
            total = dot_tn(lefts[0], rights[0]) + dot_tn(lefts[1], rights[1])
            total = total.reshape(R * A * Y, unit, -1)
            made.append(jnp.take(total, by_order, axis=0) if natural else total)
        return jnp.concatenate(made, axis=-1).reshape(width, -1).astype(bf16)

    def to_owner(dealt, widths):
        keep = lax.dynamic_index_in_dim(dealt, c, 1, keepdims=False)
        send = lax.dynamic_index_in_dim(dealt, 1 - c, 1, keepdims=False)
        return join_columns(keep, g.swap(send), spot, widths)

    def part_rows(total):
        return total.reshape(A, unit, -1)

    def core_rows(dealt):
        return dealt.reshape(A, 2, rows_own, -1)

    later = after(normed2, d_normed2)
    mlp_grad = over_tokens(
        (later, [d[0] for d in d_gu], False),
        (later, [d[1] for d in d_gu], False),
        (dout, inner, False),
    )
    mlp_total = g.scatter("by", mlp_grad)
    out_part = of_both([[v] for v in after(inner, d_normed2)], down_w)

    d_branch = grad_middle.astype(bf16)
    d_att = dot(d_branch, out_w).astype(bf16)
    if pieces * unit % LANES == 0:
        dealt = column_blocks([d_att, d_branch], A)
    else:
        dealt = jnp.concatenate([d_att.reshape(token_rows, A, -1), d_branch.reshape(token_rows, A, -1)], -1)
        dealt = jnp.swapaxes(dealt, 0, 1)
    dealt = g.exchange_a(dealt).reshape(group_rows, -1)
    d_att, rows_of_part = dealt[:, : 2 * q_cols], dealt[:, 2 * q_cols :]
    wo_total = g.scatter("byc", dot_tn(rows_of_part, att_heads).astype(bf16))
    mlp_dealt = g.exchange_a(after([part_rows(mlp_total)], d_att)[0])
    mine_half, other_half = g.by_core(d_att[:, :q_cols], d_att[:, q_cols:])
    d_att = [mine_half, g.swap(other_half)]

    def attend_back(n):
        d_mixed = d_att[n].reshape(group_rows, GROUP, HEAD_SIZE)
        o, log_total = mixed[n]
        delta = jnp.sum(jnp.transpose(d_mixed, (1, 0, 2)).astype(f32) * o, axis=-1, keepdims=True)
        q = of_sequence(query, n)
        scores = jnp.einsum("qgd,td->gqt", q, keys[n], preferred_element_type=f32)
        scores = jnp.where(visible[n], scores * score_scale, -1e30)
        weights = jnp.exp(scores - log_total)
        d_weights = jnp.einsum("qgd,td->gqt", d_mixed, values[n], preferred_element_type=f32)
        d_scores = (weights * (d_weights - delta)).astype(bf16)
        d_query = jnp.einsum("gqt,td->qgd", d_scores, keys[n], preferred_element_type=f32)
        d_key = jnp.einsum("gqt,qgd->td", d_scores, q, preferred_element_type=f32)
        d_value = jnp.einsum(
            "gqt,qgd->td", weights.astype(bf16), d_mixed, preferred_element_type=f32
        )
        return d_query * score_scale, jnp.concatenate([d_key * score_scale, d_value], axis=1)

    backs = [attend_back(0), attend_back(1)]
    d_query = jnp.concatenate([back[0] for back in backs], axis=0)
    d_kv = jnp.concatenate([of_sequence(back[1], 0) for back in backs], axis=0)
    for i in range(1, R):
        block = jnp.concatenate([of_sequence(back[1], i) for back in backs], axis=0)
        d_kv = d_kv + g.move(block.astype(bf16), b=-i).astype(f32)
    out_mine = g.scatter("a", after([out_part], mlp_dealt, wo_total, d_kv)[0])
    e_q = unrotate(d_query, cosine3, sine3)
    e_k = unrotate(d_kv[:, :HEAD_SIZE], cosine, sine)
    d_q_pre = norm_back(q_pre, q_root, query_gain, e_q).reshape(2 * group_rows, q_cols)
    d_k_pre = norm_back(k_pre, k_root, key_gain, e_k)
    qk_gain_grad = jnp.stack(
        [jnp.sum(e_q * q_pre * q_root, axis=(0, 1)), jnp.sum(e_k * k_pre * k_root, axis=0)]
    )
    d_qkv = jnp.concatenate([d_q_pre, d_k_pre, d_kv[:, HEAD_SIZE:]], axis=1).astype(bf16)
    d_qkv = [of_sequence(d_qkv, 0), of_sequence(d_qkv, 1)]
    d_qkv = after(d_qkv, mlp_dealt)
    qkv_grad = over_tokens((normed, d_qkv, True))
    d_qkv = after(d_qkv, qkv_grad)
    d_normed = of_both([[v] for v in d_qkv], qkv_w)
    qkv_total = g.scatter("by", qkv_grad)
    attn_gain_grad = jnp.sum(d_normed * inputs * x_root, axis=0)
    e1 = g.to_rows_owner(d_normed)
    grad_input = grad_middle + norm_back(
        x_own.astype(f32), inv_rms(x_own.astype(f32)), first_gain, e1
    )

    (out_sum,) = permute([out_mine.astype(f32)], True)
    result = (middle_own + out_sum).astype(bf16)
    (qkv_total,) = after([qkv_total], e1)
    dealt = core_rows(g.exchange_a(part_rows(qkv_total)))
    grad_wq, grad_wk, grad_wv = to_owner(dealt, [q_cols, HEAD_SIZE, HEAD_SIZE])

    def by_first(array):
        return jnp.swapaxes(array, 0, 1).reshape(pieces, A, 2, -1)

    small = qk_gain_grad.reshape(2, A, pieces, 2, -1)
    small = jnp.transpose(small, (2, 1, 3, 0, 4)).reshape(pieces, A, 2, -1)
    sums = jnp.concatenate(
        [
            by_first(attn_gain_grad.reshape(A, pieces, 2, rows_own)),
            by_first(mlp_gain_grad.reshape(A, pieces, 2, rows_own)),
            small,
        ],
        axis=-1,
    )
    keep = lax.dynamic_index_in_dim(sums, c, 2, keepdims=False)
    send = lax.dynamic_index_in_dim(sums, 1 - c, 2, keepdims=False)
    sums = g.collect(keep + g.swap(send))
    sums = sum(g.deal_a(g.ahead(sums)))
    sums = [
        sums[:rows_own],
        sums[rows_own : 2 * rows_own],
        sums[2 * rows_own :].reshape(2, -1),
    ]

    grad_wo = wo_total.astype(f32)
    grad_wg, grad_wu, grad_wd = to_owner(core_rows(mlp_dealt), [ff_cols] * 3)
    return (
        result[None],
        grad_input[None],
        grad_wq,
        grad_wk,
        grad_wv,
        grad_wo,
        grad_wg,
        grad_wu,
        grad_wd,
        *sums,
    )


def solution(mesh):
    placed = (
        P("fsdp", "seq", None),
        P("fsdp", None),
        P(("seq", "fsdp"), None),
        P(("seq", "fsdp"), None),
        P(("seq", "fsdp"), None),
        P(("seq", "fsdp"), None),
        P(("seq", "fsdp"), None),
        P(("seq", "fsdp"), None),
        P(("seq", "fsdp"), None),
        P(("seq", "fsdp")),
        P(("seq", "fsdp")),
        P(None, ("seq", "fsdp")),
        P("fsdp", "seq", None),
    )
    return jax.shard_map(
        on_device,
        mesh=mesh,
        in_specs=placed,
        out_specs=(
            P("fsdp", "seq", None),
            P("fsdp", "seq", None),
            P(("seq", "fsdp"), None),
            P(("seq", "fsdp"), None),
            P(("seq", "fsdp"), None),
            P(("seq", "fsdp"), None),
            P(("seq", "fsdp"), None),
            P(("seq", "fsdp"), None),
            P(("seq", "fsdp"), None),
            P(("seq", "fsdp")),
            P(("seq", "fsdp")),
            P(None, ("seq", "fsdp")),
        ),
        check_vma=False,
    )
```

```python
import jax
import jax.numpy as jnp
import numpy as np
from jax import lax
from jax.experimental import pallas as pl
from jax.experimental.pallas import tpu as pltpu
from jax.sharding import PartitionSpec as P

QUERY_HEADS = 16
KEY_VALUE_HEADS = 8
HEAD_SIZE = 128
FF = 6144

rope_base = 1000000.0
norm_eps = 1e-06
BOTH = ("seq", "fsdp")
bf16 = jnp.bfloat16
f32 = jnp.float32

PARTS = KEY_VALUE_HEADS // 2
GROUP = QUERY_HEADS // KEY_VALUE_HEADS


LANES = 128
EXTRA = 16
VMEM_BYTES = 48 * 1024 * 1024
ALL_VMEM_BYTES = 60 * 1024 * 1024


def dot(left, right):
    return jnp.dot(left, right, preferred_element_type=f32)


def dot_t(left, right):
    return lax.dot_general(left, right, (((1,), (1,)), ((), ())), preferred_element_type=f32)


def dot_tn(left, right):
    return lax.dot_general(left, right, (((0,), (0,)), ((), ())), preferred_element_type=f32)


def inv_rms(tensor):
    return lax.rsqrt(jnp.mean(tensor * tensor, axis=-1, keepdims=True) + norm_eps)


def norm_back(tensor, root, gain, incoming):
    scaled = gain * incoming
    return root * scaled - tensor * (root * root * root) * jnp.mean(
        scaled * tensor, axis=-1, keepdims=True
    )


def halves(tensor):
    half_width = tensor.shape[-1] // 2
    return tensor[..., :half_width], tensor[..., half_width:]


def rotate(tensor, cosine, sine):
    front, back = halves(tensor)
    return jnp.concatenate([front * cosine - back * sine, back * cosine + front * sine], axis=-1)


def unrotate(tensor, cosine, sine):
    front, back = halves(tensor)
    return jnp.concatenate([front * cosine + back * sine, back * cosine - front * sine], axis=-1)


class Grid:
    def __init__(self):
        self.fsdp = lax.axis_size("fsdp")
        self.A = PARTS
        self.R = lax.axis_size("seq") // self.A
        self.Y = self.fsdp // 2
        s, f = lax.axis_index("seq"), lax.axis_index("fsdp")
        self.a, self.b = s // self.R, s % self.R
        self.y, self.c = f // 2, f % 2
        self.places = [
            (a, b, y, c)
            for a in range(self.A)
            for b in range(self.R)
            for y in range(self.Y)
            for c in range(2)
        ]

    def at(self, a, b, y, c):
        return (a * self.R + b % self.R) * self.fsdp + (y % self.Y) * 2 + c % 2

    def groups(self, along):
        found = {}
        for place in self.places:
            fixed = tuple(v for v, name in zip(place, "abyc") if name not in along)
            found.setdefault(fixed, []).append(self.at(*place))
        return list(found.values())

    def move(self, array, a=0, b=0, y=0, c=0):
        route = [
            (self.at(*p), self.at(p[0] ^ a, p[1] + b, p[2] + y, p[3] + c)) for p in self.places
        ]
        return lax.ppermute(array, BOTH, route)

    def swap(self, array):
        return self.move(array, c=1)

    def exchange_a(self, array):
        return lax.all_to_all(array, BOTH, 0, 0, axis_index_groups=self.groups("a"), tiled=True)

    def gather_by(self, array):
        return lax.all_gather(array, BOTH, axis_index_groups=self.groups("by"), axis=0, tiled=True)

    def scatter(self, along, array):
        return lax.psum_scatter(
            array, BOTH, axis_index_groups=self.groups(along), scatter_dimension=0, tiled=True
        )

    def deal_a(self, blocks):
        return [blocks[0]] + [self.move(blocks[d], a=d) for d in range(1, self.A)]

    def gather_a(self, array, own_first=True, then=()):
        held = {0: array}
        bit = self.A // 2
        while bit:
            own = self.move(array, a=bit)
            rest = [d for d in held if d]
            sent = [held[d] for d in rest]
            sent = after(sent, *((own,) if own_first else then)) if rest else sent
            held[bit] = own
            held.update({d | bit: self.move(v, a=bit) for d, v in zip(rest, sent)})
            bit //= 2
        return [held[d] for d in range(self.A)]

    def ahead(self, array):
        return [
            lax.dynamic_index_in_dim(array, self.a ^ d, 0, keepdims=False) for d in range(self.A)
        ]

    def in_place(self, blocks):
        held = jnp.stack(blocks)
        return jnp.stack(
            [
                lax.dynamic_index_in_dim(held, self.a ^ part, 0, keepdims=False)
                for part in range(self.A)
            ]
        )

    def by_core(self, first, second):
        return (
            jnp.where(self.c == 0, first, second),
            jnp.where(self.c == 0, second, first),
        )

    def pairs(self):
        return [(i, j) for i in range(self.R) for j in range(self.Y)]

    def spread(self, piece):
        return [piece] + [self.move(piece, b=i, y=j) for i, j in self.pairs()[1:]]

    def mine_first(self, pieces):
        return [
            lax.dynamic_index_in_dim(
                pieces, (self.b - i) % self.R * self.Y + (self.y - j) % self.Y, 0, False
            )
            for i, j in self.pairs()
        ]

    def collect(self, pieces, *late):
        held = self.mine_first(pieces)
        got = [self.move(part, b=-i, y=-j) for part, (i, j) in zip(held[1:], self.pairs()[1:])]
        got = after(got, *late) if late else got
        return added(held[0], got)

    def to_rows_owner(self, partial):
        got = self.exchange_a(partial.reshape(self.A, -1, partial.shape[1]))
        return added(got[0], list(got[1:]))


def added(first, rest):
    total = first.astype(f32)
    for part in rest:
        total = total + part.astype(f32)
    return total


def whole_call(body, scalars, ins, outs):
    return pl.pallas_call(
        body,
        grid_spec=pltpu.PrefetchScalarGridSpec(
            num_scalar_prefetch=1,
            grid=(1,),
            in_specs=[pl.BlockSpec(v.shape, lambda i, s, n=v.ndim: (0,) * n) for v in ins],
            out_specs=[pl.BlockSpec(v.shape, lambda i, s, n=len(v.shape): (0,) * n) for v in outs],
        ),
        out_shape=outs,
        compiler_params=pltpu.CompilerParams(vmem_limit_bytes=VMEM_BYTES),
    )(scalars, *ins)


def like(shape, kind=bf16):
    return jax.ShapeDtypeStruct(shape, kind)


def at_multiple(number, size):
    return pl.ds(pl.multiple_of(number * size, size), size)


def reorder(arrays, source):
    count = len(arrays)

    def body(_, *refs):
        for i, at in enumerate(source):
            for src, dst in zip(refs[:count], refs[count:]):
                dst[:, i * LANES : (i + 1) * LANES] = src[:, at * LANES : (at + 1) * LANES]

    return whole_call(
        body, jnp.zeros((1,), jnp.int32), arrays, [like(v.shape, v.dtype) for v in arrays]
    )


def cut_columns(groups, spot, parts):
    flat = [a for group in groups for a in group]
    rows = flat[0].shape[0]
    widths = [a.shape[1] // (2 * parts) for a in flat]
    group_widths = [sum(a.shape[1] // (2 * parts) for a in group) for group in groups]

    def body(spot_ref, *refs):
        ins, outs = refs[: len(flat)], refs[len(flat) :]
        for half in range(2):
            core = spot_ref[0] if half == 0 else 1 - spot_ref[0]
            at = 0
            for k, group in enumerate(groups):
                start = 0
                for _ in group:
                    n = widths[at]
                    outs[2 * k + half][0, :, start : start + n] = ins[at][:, at_multiple(core, n)]
                    start += n
                    at += 1

    out_specs, out_shape = [], []
    for n in group_widths:
        for _ in range(2):
            out_specs.append(pl.BlockSpec((1, rows, n), lambda i, spot: (i, 0, 0)))
            out_shape.append(like((parts, rows, n)))
    made = pl.pallas_call(
        body,
        grid_spec=pltpu.PrefetchScalarGridSpec(
            num_scalar_prefetch=1,
            grid=(parts,),
            in_specs=[pl.BlockSpec((rows, 2 * n), lambda i, spot: (0, i)) for n in widths],
            out_specs=out_specs,
        ),
        out_shape=out_shape,
        compiler_params=pltpu.CompilerParams(vmem_limit_bytes=ALL_VMEM_BYTES),
    )(spot, *flat)
    return [(made[2 * k], made[2 * k + 1]) for k in range(len(groups))]


def merge_with_extra(keep, got, extras, spot):
    parts, rows, n = keep.shape
    more = extras[0].shape[0]

    def body(spot_ref, keep_ref, got_ref, own_ref, other_ref, out):
        here, there = spot_ref[0], 1 - spot_ref[0]
        for part in range(parts):
            out[part, at_multiple(here, rows), :] = keep_ref[part]
            out[part, at_multiple(there, rows), :] = got_ref[part]
            for core, ref in ((here, own_ref), (there, other_ref)):
                where = pl.ds(pl.multiple_of(2 * rows + core * more, more), more)
                out[part, where, :] = ref[...]

    return whole_call(
        body, spot, [keep, got, *extras], [like((parts, 2 * (rows + more), n))]
    )[0]


def merge_rows(keep, got, spot, widths):
    parts, rows, _ = keep.shape

    def body(spot_ref, keep_ref, got_ref, *outs):
        for part in range(parts):
            for core, ref in ((spot_ref[0], keep_ref), (1 - spot_ref[0], got_ref)):
                start = 0
                for n, out in zip(widths, outs):
                    out[part, at_multiple(core, rows), :] = ref[part, :, start : start + n]
                    start += n

    return whole_call(body, spot, [keep, got], [like((parts, 2 * rows, n)) for n in widths])


def stack_parts(blocks, spot):
    parts = len(blocks)
    rows, n = blocks[0].shape

    def body(spot_ref, *refs):
        for d in range(parts):
            refs[parts][at_multiple(spot_ref[1] ^ d, rows), :] = refs[d][...]

    return whole_call(body, spot, blocks, [like((parts * rows, n))])[0]


def stack_with_extra(blocks, where, parts, rows, more):
    n = blocks[0].shape[1]

    def body(where_ref, *refs):
        for k in range(len(blocks)):
            for part in range(parts):
                start = part * (rows + more)
                place = part * len(blocks) + where_ref[k]
                refs[-2][at_multiple(place, rows), :] = refs[k][start : start + rows, :]
                refs[-1][at_multiple(place, more), :] = refs[k][start + rows : start + rows + more, :]

    total = len(blocks) * parts
    return whole_call(body, where, blocks, [like((total * rows, n)), like((total * more, n))])


def gather_heads(blocks, spot, half):
    parts = len(blocks)
    tokens = blocks[0].shape[0]

    def body(spot_ref, *refs):
        for d in range(parts):
            for k, core in enumerate((spot_ref[0], 1 - spot_ref[0])):
                where = at_multiple(2 * (spot_ref[1] ^ d) + core, half)
                refs[-1][:, where] = refs[d][:, k * half : (k + 1) * half]

    return whole_call(body, spot, blocks, [like((tokens, 2 * parts * half))])[0]


def column_blocks(arrays, parts):
    rows = arrays[0].shape[0]
    widths = [array.shape[1] // parts for array in arrays]

    def body(_, *refs):
        for part in range(parts):
            start = 0
            for n, src in zip(widths, refs):
                refs[-1][part, :, start : start + n] = src[:, part * n : (part + 1) * n]
                start += n

    return whole_call(
        body, jnp.zeros((1,), jnp.int32), arrays, [like((parts, rows, sum(widths)))]
    )[0]


def join_columns(keep, got, spot, widths):
    parts, rows, total = keep.shape

    def body(spot_ref, keep_ref, got_ref, *outs):
        mine = pl.program_id(1) == spot_ref[0]
        start = 0
        for n, out in zip(widths, outs):
            part = slice(start, start + n)
            out[...] = jnp.where(mine, keep_ref[0, :, part], got_ref[0, :, part]).astype(f32)
            start += n

    block = pl.BlockSpec((1, rows, total), lambda i, h, spot: (i, 0, 0))
    return pl.pallas_call(
        body,
        grid_spec=pltpu.PrefetchScalarGridSpec(
            num_scalar_prefetch=1,
            grid=(parts, 2),
            in_specs=[block, block],
            out_specs=[pl.BlockSpec((rows, n), lambda i, h, spot: (0, 2 * i + h)) for n in widths],
        ),
        out_shape=[like((rows, 2 * parts * n), f32) for n in widths],
        compiler_params=pltpu.CompilerParams(vmem_limit_bytes=VMEM_BYTES),
    )(spot, keep, got)


def token_products(groups, orders):
    counts = [len(lefts) for lefts, _ in groups]
    tokens, width = groups[0][0][0].shape
    widths = [rights[0].shape[1] for _, rights in groups]
    blocks = len(orders[0])
    unit = width // blocks
    steps = min(4, blocks)
    per_step = blocks // steps

    in_turn = [bool(np.array_equal(order, np.arange(blocks))) for order in orders]

    def body(order_ref, *refs):
        at, start = 0, 0
        for m, (count, n) in enumerate(zip(counts, widths)):
            first = pl.program_id(0) * per_step
            if in_turn[m]:
                places = [at_multiple(pl.program_id(0), per_step * unit)]
            else:
                places = [
                    at_multiple(order_ref[m * blocks + first + k], unit) for k in range(per_step)
                ]
            size = per_step * unit // len(places)
            for k, where in enumerate(places):
                total = dot_tn(refs[at][:, where], refs[at + count][...])
                for i in range(1, count):
                    total = total + dot_tn(refs[at + i][:, where], refs[at + count + i][...])
                refs[-1][k * size : (k + 1) * size, start : start + n] = total.astype(bf16)
            at += 2 * count
            start += n

    flat = [v for lefts, rights in groups for v in (*lefts, *rights)]
    return pl.pallas_call(
        body,
        grid_spec=pltpu.PrefetchScalarGridSpec(
            num_scalar_prefetch=1,
            grid=(steps,),
            in_specs=[pl.BlockSpec(v.shape, lambda i, s: (0, 0)) for v in flat],
            out_specs=pl.BlockSpec((per_step * unit, sum(widths)), lambda i, s: (i, 0)),
        ),
        out_shape=like((width, sum(widths))),
        compiler_params=pltpu.CompilerParams(vmem_limit_bytes=ALL_VMEM_BYTES),
    )(jnp.asarray(np.concatenate(orders), jnp.int32), *flat)


def product_t(lefts, right, rows, add=None):
    count = len(lefts)
    tokens = lefts[0].shape[0]
    width, n = right.shape

    def body(*refs):
        right_ref = refs[count]
        total, start = None, 0
        for left in refs[:count]:
            stop = start + left.shape[1]
            part = dot_t(left[...], right_ref[:, start:stop])
            total = part if total is None else total + part
            start = stop
        if add is not None:
            total = total + refs[count + 1][...].astype(f32)
        refs[-1][...] = total.astype(bf16)

    block = pl.BlockSpec((tokens, rows), lambda i: (0, i))
    return pl.pallas_call(
        body,
        grid=(width // rows,),
        in_specs=[pl.BlockSpec(left.shape, lambda i: (0, 0)) for left in lefts]
        + [pl.BlockSpec((rows, n), lambda i: (i, 0))]
        + ([] if add is None else [block]),
        out_specs=block,
        out_shape=like((tokens, width)),
        compiler_params=pltpu.CompilerParams(vmem_limit_bytes=ALL_VMEM_BYTES),
    )(*lefts, right, *([] if add is None else [add]))


def feed_forward(normed, gate_up, dout, down):
    tokens, width = normed.shape
    units = down.shape[1]
    cols = 256
    steps = units // cols

    def body(normed_ref, gate_ref, up_ref, dout_ref, down_ref, inner_ref, d_gate_ref, d_up_ref):
        gate = dot(normed_ref[...], gate_ref[...])
        up = dot(normed_ref[...], up_ref[...])
        d_inner = dot(dout_ref[...], down_ref[...])
        s = jax.nn.sigmoid(gate)
        act = gate * s
        inner_ref[...] = (act * up).astype(bf16)
        d_gate_ref[...] = (d_inner * up * s * (1.0 + gate * (1.0 - s))).astype(bf16)
        d_up_ref[...] = (d_inner * act).astype(bf16)

    rows = pl.BlockSpec((tokens, width), lambda i: (0, 0))
    block = pl.BlockSpec((tokens, cols), lambda i: (0, i))
    return pl.pallas_call(
        body,
        grid=(steps,),
        in_specs=[
            rows,
            pl.BlockSpec((width, cols), lambda i: (0, i)),
            pl.BlockSpec((width, cols), lambda i: (0, steps + i)),
            rows,
            pl.BlockSpec((width, cols), lambda i: (0, i)),
        ],
        out_specs=[block] * 3,
        out_shape=[like((tokens, units))] * 3,
        compiler_params=pltpu.CompilerParams(vmem_limit_bytes=ALL_VMEM_BYTES),
    )(normed, gate_up, gate_up, dout, down)


def after(values, *others):
    return list(lax.optimization_barrier(tuple(values) + others))[: len(values)]


def on_device(
    tokens,
    block_pos,
    w_query,
    key_weight,
    value_weight,
    w_out,
    w_gate,
    w_up,
    w_down,
    attn_gain,
    mlp_gain,
    qk_gain,
    grad_out,
):
    g = Grid()
    A, R, Y = g.A, g.R, g.Y
    a, b, y, c = g.a, g.b, g.y, g.c
    pieces = R * Y
    rows_own = w_query.shape[0]
    width = tokens.shape[2]
    piece_width = width // pieces
    token_rows = tokens.shape[1]
    group_rows = A * token_rows
    score_scale = HEAD_SIZE ** (-0.5)
    q_cols = GROUP * HEAD_SIZE
    qkv_cols = q_cols + 2 * HEAD_SIZE
    ff_cols = FF // (2 * A)
    spot = jnp.stack([c, a]).astype(jnp.int32)

    unit = 2 * rows_own

    def permute(arrays, back):
        cuts = (R * Y, A, unit) if back else (A, R * Y, unit)
        columns = np.arange(width).reshape(cuts).transpose(1, 0, 2).reshape(-1)
        if unit % LANES == 0:
            return reorder(arrays, (columns[::LANES] // LANES).tolist())
        return [jnp.take(array, columns, axis=1) for array in arrays]

    places = jnp.stack(
        [(b - i) % R * Y + (y - j) % Y for i, j in g.pairs()]
    ).astype(jnp.int32)

    x_own, dout_own = tokens[0], grad_out[0]
    x_parts = g.gather_a(x_own, own_first=False)
    out_w = lax.all_gather(w_out, BOTH, axis=0, tiled=True)
    (cut,) = cut_columns([[w_query, key_weight, value_weight]], spot, A)
    packed = jnp.concatenate([attn_gain, mlp_gain, qk_gain.reshape(-1)])
    packed = jnp.stack(
        [jnp.pad(v, (0, qkv_cols - v.shape[0])) for v in (packed, block_pos[0].astype(bf16))]
    )
    packed = jnp.pad(packed, ((0, EXTRA - 2), (0, 0)))
    sent = jnp.concatenate([cut[1].reshape(A * rows_own, qkv_cols), packed])
    got = g.swap(sent)
    other_packed = got[A * rows_own :]
    qkv_local = merge_with_extra(
        cut[0],
        got[: A * rows_own].reshape(A, rows_own, qkv_cols),
        [packed, other_packed],
        spot,
    )
    qkv_piece = g.exchange_a(qkv_local).reshape(-1, qkv_cols)
    qkv_w, extras = stack_with_extra(g.spread(qkv_piece), places, A, unit, 2 * EXTRA)
    packed = extras.reshape(2 * A * pieces, EXTRA, qkv_cols)[:, 0].astype(f32)
    first_gain = packed[..., :rows_own].reshape(width)
    second_gain = packed[..., rows_own : 2 * rows_own].reshape(width)
    small = packed[..., 2 * rows_own : 2 * rows_own + 2 * (HEAD_SIZE // (2 * pieces * A))]
    small = jnp.transpose(small.reshape(2 * A * pieces, 2, -1), (1, 0, 2)).reshape(2, HEAD_SIZE)
    query_gain, key_gain = small[0], small[1]

    (cut,) = cut_columns([[w_gate, w_up, w_down]], after([spot], qkv_local)[0], A)
    gu_local, down_local = merge_rows(cut[0], g.swap(cut[1]), spot, [2 * ff_cols, ff_cols])
    (gu_local,) = after([gu_local], qkv_piece)
    gu_piece = g.exchange_a(gu_local).reshape(A * unit, 2 * ff_cols)
    (down_local,) = after([down_local], gu_piece)
    down_piece = g.exchange_a(down_local).reshape(A * unit, ff_cols)

    blocks_seen = block_pos.shape[1]
    orders = [block_pos[0], other_packed[1, :blocks_seen].astype(jnp.int32)]
    row_offsets = jnp.arange(token_rows, dtype=jnp.int32)

    def positions(order, shift):
        blocks = [order[part * R + (b - shift) % R] for part in range(A)]
        return jnp.concatenate([block * token_rows + row_offsets for block in blocks])

    local_pos = [positions(order, 0) for order in orders]
    key_pos = [jnp.concatenate([positions(order, i) for i in range(R)]) for order in orders]
    exponent = jnp.arange(HEAD_SIZE // 2, dtype=f32) * (-2.0 / HEAD_SIZE)
    angles = jnp.concatenate(local_pos).astype(f32)[:, None] * (rope_base**exponent)[None, :]
    cosine, sine = jnp.cos(angles), jnp.sin(angles)
    cosine3, sine3 = cosine[:, None, :], sine[:, None, :]

    x_group = stack_parts(x_parts, spot)
    inputs = x_group.astype(f32)
    x_root = inv_rms(inputs)
    normed_own = (inputs * x_root * first_gain).astype(bf16)
    normed = [normed_own, g.swap(normed_own)]
    made = jnp.concatenate([dot(part, qkv_w) for part in normed], axis=0)
    gu_by = g.gather_by(after([gu_piece], out_w, made)[0])
    down_w = g.gather_by(after([down_piece], gu_by)[0])
    q_pre = made[:, :q_cols].reshape(2 * group_rows, GROUP, HEAD_SIZE)
    k_pre = made[:, q_cols : q_cols + HEAD_SIZE]
    value = made[:, q_cols + HEAD_SIZE :].astype(bf16)
    q_root, k_root = inv_rms(q_pre), inv_rms(k_pre)
    query = rotate(q_pre * q_root * query_gain, cosine3, sine3).astype(bf16)
    key = rotate(k_pre * k_root * key_gain, cosine, sine).astype(bf16)
    key_values = jnp.concatenate([key, value], axis=1)
    key_values = [key_values] + [g.move(key_values, b=i) for i in range(1, R)]

    def of_sequence(array, n):
        return array[n * group_rows : (n + 1) * group_rows]

    keys = [
        jnp.concatenate([of_sequence(kv, n)[:, :HEAD_SIZE] for kv in key_values]) for n in range(2)
    ]
    values = [
        jnp.concatenate([of_sequence(kv, n)[:, HEAD_SIZE:] for kv in key_values]) for n in range(2)
    ]

    visible = [local_pos[n][:, None] >= key_pos[n][None, :] for n in range(2)]

    def attend(n):
        scores = jnp.einsum(
            "qgd,td->gqt", of_sequence(query, n), keys[n], preferred_element_type=f32
        )
        scores = jnp.where(visible[n], scores * score_scale, -1e30)
        top = jnp.max(scores, axis=-1, keepdims=True)
        weights = jnp.exp(scores - top)
        totals = jnp.sum(weights, axis=-1, keepdims=True)
        log_total = top + jnp.log(totals)
        mixed = jnp.einsum(
            "gqt,td->gqd", weights.astype(bf16), values[n], preferred_element_type=f32
        )
        return mixed / totals, log_total

    def flat(heads):
        return jnp.transpose(heads, (1, 0, 2)).reshape(group_rows, q_cols).astype(bf16)

    mixed_other = attend(1)
    got = g.swap(flat(mixed_other[0]))
    mixed = [attend(0), mixed_other]
    attended = jnp.concatenate([flat(mixed[0][0]), got], axis=1)
    (attended,) = after([attended], down_piece)
    att_parts = g.gather_a(attended)
    att_heads = gather_heads(after(att_parts, gu_by), spot, q_cols)

    (dout_by,) = permute(after([dout_own], att_parts[-1]), False)
    middle = inputs + dot_t(att_heads, out_w)
    dout_parts = g.gather_a(dout_by, False, (middle,))
    root2 = inv_rms(middle)
    normed2_own = (middle * root2 * second_gain).astype(bf16)
    (normed2_own,) = permute([normed2_own], False)
    normed2 = [normed2_own, g.swap(normed2_own)]
    dout_group = stack_parts(dout_parts, spot)
    dout = [dout_group, g.swap(dout_group)]
    fed = [feed_forward(normed2[n], gu_by, dout[n], down_w) for n in range(2)]
    inner = [f[0] for f in fed]
    d_gu = [f[1:] for f in fed]

    def of_both(parts, weight):
        got = g.swap(product_t(parts[1], weight, 512))
        return product_t(parts[0], weight, 512, got)

    def own_rows(array):
        return lax.dynamic_slice_in_dim(array, a * token_rows, token_rows, axis=0)

    d_normed2 = of_both(d_gu, gu_by)
    (e2,) = permute([g.to_rows_owner(d_normed2)], True)
    middle_own, root2_own = own_rows(middle), own_rows(root2)
    mlp_gain_grad = jnp.sum(e2 * middle_own * root2_own, axis=0)
    grad_middle = dout_own.astype(f32) + norm_back(middle_own, root2_own, second_gain, e2)

    by_order = np.arange(R * A * Y).reshape(A, R * Y).T.reshape(-1)

    def over_tokens(*groups):
        if unit % LANES == 0:
            orders = [by_order if natural else np.arange(R * A * Y) for _, _, natural in groups]
            return token_products([group[:2] for group in groups], orders)
        made = []
        for lefts, rights, natural in groups:
            total = dot_tn(lefts[0], rights[0]) + dot_tn(lefts[1], rights[1])
            total = total.reshape(R * A * Y, unit, -1)
            made.append(jnp.take(total, by_order, axis=0) if natural else total)
        return jnp.concatenate(made, axis=-1).reshape(width, -1).astype(bf16)

    def to_owner(dealt, widths):
        keep = lax.dynamic_index_in_dim(dealt, c, 1, keepdims=False)
        send = lax.dynamic_index_in_dim(dealt, 1 - c, 1, keepdims=False)
        return join_columns(keep, g.swap(send), spot, widths)

    def part_rows(total):
        return total.reshape(A, unit, -1)

    def core_rows(dealt):
        return dealt.reshape(A, 2, rows_own, -1)

    later = after(normed2, d_normed2)
    mlp_grad = over_tokens(
        (later, [d[0] for d in d_gu], False),
        (later, [d[1] for d in d_gu], False),
        (dout, inner, False),
    )
    mlp_total = g.scatter("by", mlp_grad)
    out_part = of_both([[v] for v in after(inner, d_normed2)], down_w)

    d_branch = grad_middle.astype(bf16)
    d_att = dot(d_branch, out_w).astype(bf16)
    if pieces * unit % LANES == 0:
        dealt = column_blocks([d_att, d_branch], A)
    else:
        dealt = jnp.concatenate([d_att.reshape(token_rows, A, -1), d_branch.reshape(token_rows, A, -1)], -1)
        dealt = jnp.swapaxes(dealt, 0, 1)
    dealt = g.exchange_a(dealt).reshape(group_rows, -1)
    d_att, rows_of_part = dealt[:, : 2 * q_cols], dealt[:, 2 * q_cols :]
    wo_total = g.scatter("byc", dot_tn(rows_of_part, att_heads).astype(bf16))
    mlp_dealt = g.exchange_a(after([part_rows(mlp_total)], d_att)[0])
    mine_half, other_half = g.by_core(d_att[:, :q_cols], d_att[:, q_cols:])
    d_att = [mine_half, g.swap(other_half)]

    def attend_back(n):
        d_mixed = d_att[n].reshape(group_rows, GROUP, HEAD_SIZE)
        o, log_total = mixed[n]
        delta = jnp.sum(jnp.transpose(d_mixed, (1, 0, 2)).astype(f32) * o, axis=-1, keepdims=True)
        q = of_sequence(query, n)
        scores = jnp.einsum("qgd,td->gqt", q, keys[n], preferred_element_type=f32)
        scores = jnp.where(visible[n], scores * score_scale, -1e30)
        weights = jnp.exp(scores - log_total)
        d_weights = jnp.einsum("qgd,td->gqt", d_mixed, values[n], preferred_element_type=f32)
        d_scores = (weights * (d_weights - delta)).astype(bf16)
        d_query = jnp.einsum("gqt,td->qgd", d_scores, keys[n], preferred_element_type=f32)
        d_key = jnp.einsum("gqt,qgd->td", d_scores, q, preferred_element_type=f32)
        d_value = jnp.einsum(
            "gqt,qgd->td", weights.astype(bf16), d_mixed, preferred_element_type=f32
        )
        return d_query * score_scale, jnp.concatenate([d_key * score_scale, d_value], axis=1)

    backs = [attend_back(0), attend_back(1)]
    d_query = jnp.concatenate([back[0] for back in backs], axis=0)
    d_kv = jnp.concatenate([of_sequence(back[1], 0) for back in backs], axis=0)
    for i in range(1, R):
        block = jnp.concatenate([of_sequence(back[1], i) for back in backs], axis=0)
        d_kv = d_kv + g.move(block.astype(bf16), b=-i).astype(f32)
    out_mine = g.scatter("a", after([out_part], mlp_dealt, wo_total, d_kv)[0])
    e_q = unrotate(d_query, cosine3, sine3)
    e_k = unrotate(d_kv[:, :HEAD_SIZE], cosine, sine)
    d_q_pre = norm_back(q_pre, q_root, query_gain, e_q).reshape(2 * group_rows, q_cols)
    d_k_pre = norm_back(k_pre, k_root, key_gain, e_k)
    qk_gain_grad = jnp.stack(
        [jnp.sum(e_q * q_pre * q_root, axis=(0, 1)), jnp.sum(e_k * k_pre * k_root, axis=0)]
    )
    d_qkv = jnp.concatenate([d_q_pre, d_k_pre, d_kv[:, HEAD_SIZE:]], axis=1).astype(bf16)
    d_qkv = [of_sequence(d_qkv, 0), of_sequence(d_qkv, 1)]
    d_qkv = after(d_qkv, mlp_dealt)
    qkv_grad = over_tokens((normed, d_qkv, True))
    d_qkv = after(d_qkv, qkv_grad)
    d_normed = of_both([[v] for v in d_qkv], qkv_w)
    qkv_total = g.scatter("by", qkv_grad)
    attn_gain_grad = jnp.sum(d_normed * inputs * x_root, axis=0)
    e1 = g.to_rows_owner(d_normed)
    grad_input = grad_middle + norm_back(
        x_own.astype(f32), inv_rms(x_own.astype(f32)), first_gain, e1
    )

    (out_sum,) = permute([out_mine.astype(f32)], True)
    result = (middle_own + out_sum).astype(bf16)
    (qkv_total,) = after([qkv_total], e1)
    dealt = core_rows(g.exchange_a(part_rows(qkv_total)))
    grad_wq, grad_wk, grad_wv = to_owner(dealt, [q_cols, HEAD_SIZE, HEAD_SIZE])

    def by_first(array):
        return jnp.swapaxes(array, 0, 1).reshape(pieces, A, 2, -1)

    small = qk_gain_grad.reshape(2, A, pieces, 2, -1)
    small = jnp.transpose(small, (2, 1, 3, 0, 4)).reshape(pieces, A, 2, -1)
    sums = jnp.concatenate(
        [
            by_first(attn_gain_grad.reshape(A, pieces, 2, rows_own)),
            by_first(mlp_gain_grad.reshape(A, pieces, 2, rows_own)),
            small,
        ],
        axis=-1,
    )
    keep = lax.dynamic_index_in_dim(sums, c, 2, keepdims=False)
    send = lax.dynamic_index_in_dim(sums, 1 - c, 2, keepdims=False)
    sums = g.collect(keep + g.swap(send))
    sums = sum(g.deal_a(g.ahead(sums)))
    sums = [
        sums[:rows_own],
        sums[rows_own : 2 * rows_own],
        sums[2 * rows_own :].reshape(2, -1),
    ]

    grad_wo = wo_total.astype(f32)
    grad_wg, grad_wu, grad_wd = to_owner(core_rows(mlp_dealt), [ff_cols] * 3)
    return (
        result[None],
        grad_input[None],
        grad_wq,
        grad_wk,
        grad_wv,
        grad_wo,
        grad_wg,
        grad_wu,
        grad_wd,
        *sums,
    )


def solution(mesh):
    placed = (
        P("fsdp", "seq", None),
        P("fsdp", None),
        P(("seq", "fsdp"), None),
        P(("seq", "fsdp"), None),
        P(("seq", "fsdp"), None),
        P(("seq", "fsdp"), None),
        P(("seq", "fsdp"), None),
        P(("seq", "fsdp"), None),
        P(("seq", "fsdp"), None),
        P(("seq", "fsdp")),
        P(("seq", "fsdp")),
        P(None, ("seq", "fsdp")),
        P("fsdp", "seq", None),
    )
    return jax.shard_map(
        on_device,
        mesh=mesh,
        in_specs=placed,
        out_specs=(
            P("fsdp", "seq", None),
            P("fsdp", "seq", None),
            P(("seq", "fsdp"), None),
            P(("seq", "fsdp"), None),
            P(("seq", "fsdp"), None),
            P(("seq", "fsdp"), None),
            P(("seq", "fsdp"), None),
            P(("seq", "fsdp"), None),
            P(("seq", "fsdp"), None),
            P(("seq", "fsdp")),
            P(("seq", "fsdp")),
            P(None, ("seq", "fsdp")),
        ),
        check_vma=False,
    )
```
